32 devices in a mesh: grp: 2 (over x), store: 16 (over z, y, core).
Axes of the slice: x: 2, y: 2, z: 4, core: 2. Of those that a mesh axis runs over, the one named last changes fastest.
Arguments:
- query_inputs: bfloat16 [128, 16, 4096], P(('grp', 'store')), parts along dimension 0, may hold values from -6 to 6
- query_grads: bfloat16 [128, 16, 4096], P(('grp', 'store')), parts along dimension 0, may hold values from -0.099609375 to 0.099609375
- hash_in: int32 [4096], replicated, may hold values from 0 to 4095
- sign_in: int32 [4096], replicated, may hold values from 0 to 1
- hash_out: int32 [4096], replicated, may hold values from 0 to 4095
- sign_out: int32 [4096], replicated, may hold values from 0 to 1
- stored: bfloat16 [128, 4096], P(('grp', 'store')), parts along dimension 0, may hold values from -0.099609375 to 0.099609375
Outputs:
- scores: float32 [128, 64], P(('grp', 'store')), parts along dimension 0
- influence: float32 [128], P(('grp', 'store')), parts along dimension 0
The draws below stay inside these ranges and needn't reach their ends.
There are 2 independent parts, one for each index of `grp`. The reference program is written for one: setup_inputs(seed, part) draws one part's arguments, and reference() takes and returns one part's arrays. A program takes and returns all parts, laid end to end along the dimension named above; an argument that names none is the same for every part. Nothing has to cross between parts.
All inputs are finite; a program needn't handle non-finite values.
Results may differ from the reference program's by a relative error of at most 0.0029.
Values may be sent and summed in bfloat16 or wider, within the bound.
No kernel may reach another device: no remote copies, remote signals or barrier semaphores. Data moves between devices by JAX's collectives and lax.ppermute only.
A program may use at most 64 MiB of HBM per device.

```python
import jax
import jax.numpy as jnp
from jax import lax

DIN = 4096
DOUT = 4096
K = 4096
TOKQ = 16
QUERIES = 64
EXAMPLES = 64


def with_ends(array, stream_key, smallest, high):
    longest = array.shape.index(max(array.shape))
    spots = []
    for shift in (0, 1):
        where = [jax.random.randint(jax.random.fold_in(stream_key, axis), (), 0, length) for axis, length in enumerate(array.shape)]
        where[longest] = (where[longest] + shift) % array.shape[longest]
        spots.append(tuple(where))
    return array.at[spots[0]].set(smallest).at[spots[1]].set(high)


def block_levels(rng, dims, shards, smallest, largest):
    loudness = 1.0
    for position, parts in shards:
        steps = jax.random.uniform(jax.random.fold_in(jax.random.fold_in(rng, 6), position), (parts,), jnp.float32, smallest / len(shards), largest / len(shards))
        loudness = loudness * jnp.repeat(jnp.exp(steps), dims[position] // parts).reshape((-1,) + (1,) * (len(dims) - 1 - position))
    return loudness


def noise(stream_key, shape, deviation, most, split=(), held_as=jnp.bfloat16):
    entries = deviation * jax.random.normal(stream_key, shape, jnp.float32)
    if split:
        entries = entries * block_levels(stream_key, shape, split, -0.22, 0.18)
    return jnp.clip(entries, -most, most).astype(held_as)


def setup_inputs(seed: int = 0, part: int = 0) -> dict:
    keys = jax.random.split(jax.random.key(seed), 8)
    part_splits = jax.random.split(jax.random.fold_in(keys[7], part), 8)
    query_inputs = noise(part_splits[0], (QUERIES, TOKQ, DIN), 1.0, 6.0, ((0, 16),))
    query_grads = noise(part_splits[1], (QUERIES, TOKQ, DOUT), 0.015625, 0.099609375, ((0, 16),))
    hash_in = with_ends(jax.random.randint(keys[2], (DIN,), 0, K), jax.random.fold_in(keys[2], 1), 0, K - 1).astype(jnp.int32)
    sign_in = with_ends(jax.random.randint(keys[3], (DIN,), 0, 2), jax.random.fold_in(keys[3], 1), 0, 1).astype(jnp.int32)
    hash_out = with_ends(jax.random.randint(keys[4], (DOUT,), 0, K), jax.random.fold_in(keys[4], 1), 0, K - 1).astype(jnp.int32)
    sign_out = with_ends(jax.random.randint(keys[5], (DOUT,), 0, 2), jax.random.fold_in(keys[5], 1), 0, 1).astype(jnp.int32)
    stored = noise(part_splits[6], (EXAMPLES, K), 0.015625, 0.099609375, ((0, 16),))
    return {"query_inputs": query_inputs, "query_grads": query_grads, "hash_in": hash_in, "sign_in": sign_in, "hash_out": hash_out, "sign_out": sign_out, "stored": stored}


def count_table(hashes, signs):
    columns = lax.iota(jnp.int32, K)
    signed = (2 * signs - 1).astype(jnp.float32)[:, None]
    hits = (hashes.astype(jnp.int32)[:, None] == columns[None, :]).astype(jnp.float32)
    return (hits * signed).astype(jnp.bfloat16)


def reference(query_inputs, query_grads, hash_in, sign_in, hash_out, sign_out, stored):
    in_table = count_table(hash_in, sign_in)
    out_table = count_table(hash_out, sign_out)

    def one_query(pair):
        inputs_one, grads_one = pair
        input_count = jnp.dot(inputs_one, in_table, preferred_element_type=jnp.float32)
        grad_count = jnp.dot(grads_one, out_table, preferred_element_type=jnp.float32)
        input_freq = jnp.fft.fft(input_count, axis=1)
        grad_freq = jnp.fft.fft(grad_count, axis=1)
        product = jnp.sum(input_freq * grad_freq, axis=0)
        return jnp.real(jnp.fft.ifft(product)).astype(jnp.float32)

    convolved = lax.map(one_query, (query_inputs, query_grads))
    sketches = convolved.astype(jnp.bfloat16)
    scores = jnp.dot(sketches, stored.T, preferred_element_type=jnp.float32)
    influence = jnp.sum(scores, axis=0) / QUERIES
    return scores, influence
```

```python
import functools, math
import numpy as np
import jax, jax.numpy as jnp
from jax import lax
from jax.sharding import PartitionSpec as P
from jax.experimental import pallas as pl
from jax.experimental.pallas import tpu as pltpu
bf=jnp.bfloat16; f32=jnp.float32
NT=(((1,),(1,)),((),()))

def rfft(x):
    n=len(x)
    if n==1: return [(x[0],None)]
    if n==2: return [(x[0]+x[1],None),(x[0]-x[1],None)]
    e=rfft(x[0::2]); o=rfft(x[1::2]); h=n//2; out=[None]*(h+1)
    out[0]=(e[0][0]+o[0][0],None); out[h]=(e[0][0]-o[0][0],None)
    for k in range(1,h//2):
        c,s=math.cos(2*math.pi*k/n),math.sin(2*math.pi*k/n)
        re,im=o[k]
        if 8*k==n:
            tr=(re+im)*c; ti=(im-re)*c
        else:
            tr=re*c+im*s; ti=im*c-re*s
        out[k]=(e[k][0]+tr,e[k][1]+ti); out[h-k]=(e[k][0]-tr,ti-e[k][1])
    out[h//2]=(e[h//2][0],-o[h//2][0])
    return out

def irfft(X):
    h=len(X)-1; n=2*h
    if h==0: return [X[0][0]]
    if h==1: return [X[0][0]+X[1][0],X[0][0]-X[1][0]]
    E=[None]*(h//2+1); O=[None]*(h//2+1)
    E[0]=(X[0][0]+X[h][0],None); O[0]=(X[0][0]-X[h][0],None)
    for k in range(1,h//2):
        c,s=math.cos(2*math.pi*k/n),math.sin(2*math.pi*k/n)
        (ar,ai),(br,bi)=X[k],X[h-k]
        E[k]=(ar+br,ai-bi)
        dr,di=ar-br,ai+bi
        if 8*k==n: O[k]=((dr-di)*c,(dr+di)*c)
        else: O[k]=(dr*c-di*s,dr*s+di*c)
    r,i=X[h//2]
    E[h//2]=(2.0*r,None); O[h//2]=(-2.0*i,None)
    ev=irfft(E); od=irfft(O); out=[None]*n
    out[0::2]=ev; out[1::2]=od
    return out

def split(z):
    hi=z.astype(bf); return hi,(z-hi.astype(f32)).astype(bf)

def tables(A,W):
    i=np.arange(W); ang=2*np.pi*(np.outer(i,i)%W)/W
    cs=np.concatenate([np.cos(ang),np.sin(ang)],1).astype(np.float32)
    hi=cs.astype(jnp.bfloat16); lo=(cs-hi.astype(np.float32)).astype(jnp.bfloat16)
    n=np.arange(A//2+1); t=2*np.pi*np.outer(n,i)/(A*W)
    tw=np.concatenate([np.cos(t),np.sin(t)],0).astype(np.float32)
    pad=-tw.shape[0]%8
    return np.concatenate([hi,lo],0), np.concatenate([tw,np.zeros((pad,W),np.float32)],0)

def count_block(x_ref, h_ref, s_ref, lo, hi, A, W):
    ls=[]; bs=[]
    for j in range(lo//128, hi//128):
        h=h_ref[j:j+1,:]; sg=(2*s_ref[j:j+1,:]-1).astype(f32).astype(bf)
        a=lax.shift_right_logical(h,int(math.log2(W))).astype(f32).astype(bf)
        b=(h&(W-1)).astype(f32).astype(bf)
        xs=x_ref[:,j*128:(j+1)*128]*sg
        z=jnp.zeros_like(xs)
        ab=jnp.broadcast_to(a,xs.shape)
        ls.append(jnp.concatenate([jnp.where(ab==jnp.asarray(k,bf),xs,z) for k in range(A)],0))
        it=lax.broadcasted_iota(jnp.int32,(W,128),0).astype(f32).astype(bf)
        bs.append(jnp.where(it==jnp.broadcast_to(b,(W,128)),jnp.ones((W,128),bf),jnp.zeros((W,128),bf)))
    return jnp.concatenate(ls,1), jnp.concatenate(bs,1)

def counts(x_ref,h_ref,s_ref,o_ref,chunk,A,W):
    for c in range(0,x_ref.shape[1],chunk):
        l,b=count_block(x_ref,h_ref,s_ref,c,c+chunk,A,W)
        p=lax.dot_general(l,b,NT,preferred_element_type=f32)
        if c==0: o_ref[...]=p
        else: o_ref[...]+=p

def dft3(hi,lo,cs):
    W=cs.shape[0]//2
    dot=functools.partial(jnp.dot,preferred_element_type=f32)
    return dot(hi,cs[:W,:])+(dot(lo,cs[:W,:])+dot(hi,cs[W:,:]))

def forward_rows(cnt,tw,hi_s,lo_s,R,A,W,which):
    H=A//2+1
    for r in range(0,R,8):
        X=rfft([cnt[k*R+r:k*R+r+8,:] for k in range(A)])
        for n,(re,im) in enumerate(X):
            if n:
                c=tw[n:n+1,:]; s=tw[H+n:H+n+1,:]
                if im is None: re,im=re*c,-re*s
                else: re,im=re*c+im*s,im*c-re*s
            for p,v in ((0,re),(1,im)):
                if v is None: continue
                yield n,p,r,v

def kernel(x_hbm,y_hbm,hi_hbm,si_hbm,ho_hbm,so_hbm,cs_hbm,tw_hbm,o_ref,
           x,y,hin,sin_,hout,sout,cs,tw,cx,cy,zh,zl,sem,*,Q,T,A,W,chunk):
    R=Q*T; H=A//2+1
    cps=[pltpu.make_async_copy(s,d,sem.at[i]) for i,(s,d) in enumerate(
        ((x_hbm,x),(hi_hbm,hin),(si_hbm,sin_),(y_hbm,y),(ho_hbm,hout),(so_hbm,sout),(cs_hbm,cs),(tw_hbm,tw)))]
    for c in cps: c.start()
    for c in cps[:3]: c.wait()
    counts(x,hin,sin_,cx,chunk,A,W)
    for c in cps[3:6]: c.wait()
    counts(y,hout,sout,cy,chunk,A,W)
    for c in cps[6:]: c.wait()
    prods=[]
    for w,cnt in ((0,cx),(1,cy)):
        for n,p,r,v in forward_rows(cnt,tw,zh,zl,R,A,W,w):
            base=((n*4)+w*2+p)*R+r
            h=v.astype(bf)
            zh[base:base+8,:]=v
    for n in range(H):
        if n==0:
            parts=[]
            U=[]
            for w in (0,1):
                v=zh[(n*4+w*2)*R:(n*4+w*2+1)*R,:]
                U.append(v)
            z=jnp.concatenate(U,0)
        else:
            z=zh[n*4*R:(n+1)*4*R,:]
        u=dft3(*split(z),cs)
        if n==0:
            ar,ai=u[:R,:W],-u[:R,W:]
            br,bi=u[R:,:W],-u[R:,W:]
        else:
            ar=u[:R,:W]+u[R:2*R,W:]; ai=u[R:2*R,:W]-u[:R,W:]
            br=u[2*R:3*R,:W]+u[3*R:,W:]; bi=u[3*R:,:W]-u[2*R:3*R,W:]
        pr=ar*br-ai*bi; pi=ar*bi+ai*br
        prods.append(pr.reshape(Q,T,W).sum(1)); prods.append(pi.reshape(Q,T,W).sum(1))
    z=jnp.concatenate(prods,0)*(1.0/(A*W))
    u=dft3(*split(z),cs)
    X=[]
    for n in range(H):
        a=u[2*n*Q:(2*n+1)*Q]; b=u[(2*n+1)*Q:(2*n+2)*Q]
        re=a[:,:W]-b[:,W:]; im=b[:,:W]+a[:,W:]
        if n==0: X.append((re,None)); continue
        c=tw[n:n+1,:]; s=tw[H+n:H+n+1,:]
        if n==A//2: X.append((re*c-im*s,None))
        else: X.append((re*c-im*s,re*s+im*c))
    out=irfft(X)
    for k in range(A):
        o_ref[:,k*W:(k+1)*W]=out[k].astype(o_ref.dtype)

def sketch(x,y,hin,sin_,hout,sout,K,*,A=16,chunk=256):
    Q,T,D=x.shape; Do=y.shape[2]; W=K//A; R=Q*T; H=A//2+1
    cs,tw=tables(A,W)
    cs=jnp.asarray(cs); tw=jnp.asarray(tw)
    x=x.reshape(R,D); y=y.reshape(R,Do)
    hs=[v.reshape(-1,128) for v in (hin,sin_,hout,sout)]
    any_=pl.BlockSpec(memory_space=pl.ANY)
    return pl.pallas_call(functools.partial(kernel,Q=Q,T=T,A=A,W=W,chunk=chunk),
        out_shape=jax.ShapeDtypeStruct((Q,K),bf),
        in_specs=[any_]*8,out_specs=pl.BlockSpec(memory_space=pltpu.VMEM),
        scratch_shapes=[pltpu.VMEM(x.shape,bf),pltpu.VMEM(y.shape,bf),
            *[pltpu.VMEM(v.shape,v.dtype) for v in hs],
            pltpu.VMEM(cs.shape,cs.dtype),pltpu.VMEM(tw.shape,tw.dtype),
            pltpu.VMEM((A*R,W),f32),pltpu.VMEM((A*R,W),f32),
            pltpu.VMEM((H*4*R,W),f32),pltpu.VMEM((8,128),bf),
            pltpu.SemaphoreType.DMA((8,))],
        compiler_params=pltpu.CompilerParams(vmem_limit_bytes=60<<20))(x,y,*hs,cs,tw)


def swap(v, bit, n):
    return lax.ppermute(v, "store", [(i, i ^ bit) for i in range(n)])


def bits_of(n):
    return [1 << b for b in range(1, n.bit_length() - 1)] + [1]


def body(query_inputs, query_grads, hash_in, sign_in, hash_out, sign_out, stored):
    n = lax.axis_size("store")
    q_dev = query_inputs.shape[0]
    me = lax.axis_index("store")
    rows = stored[None]
    for bit in bits_of(n):
        other = swap(rows, bit, n)
        rows = jnp.concatenate([rows, other], 0)
    sk = sketch(query_inputs, query_grads, hash_in, sign_in, hash_out, sign_out, stored.shape[1])
    e = stored.shape[0]
    s = lax.dot_general(sk, rows.reshape(n * e, -1), NT, preferred_element_type=f32)
    s = s.reshape((q_dev,) + (2,) * (n.bit_length() - 1) + (e,))
    order = bits_of(n)[::-1]
    for pos, bit in enumerate(order):
        s = jnp.where((me & bit) != 0, jnp.flip(s, 1 + pos), s)
    where = {bit: 1 + pos for pos, bit in enumerate(order)}
    axes = [where[1 << b] for b in reversed(range(n.bit_length() - 1))]
    s = s.transpose([0] + axes + [s.ndim - 1]).reshape(q_dev, n * e)
    t = jnp.sum(s, 0)
    for bit in [1] + bits_of(n)[:-1]:
        t = t + swap(t, bit, n)
    t = lax.dynamic_slice_in_dim(t, me * e, e, 0)
    return s, t / (n * q_dev)


def solution(mesh):
    rows = P(("grp", "store"), None)
    cube = P(("grp", "store"), None, None)
    return jax.shard_map(body, mesh=mesh, in_specs=(cube, cube, P(), P(), P(), P(), rows),
        out_specs=(rows, P(("grp", "store"))), check_vma=False)
```

```python
import functools, math
import numpy as np
import jax, jax.numpy as jnp
from jax import lax
from jax.experimental import pallas as pl
from jax.experimental.pallas import tpu as pltpu
from jax.sharding import PartitionSpec as P

bf = jnp.bfloat16
f32 = jnp.float32
NT = (((1,), (1,)), ((), ()))
VMEM_LIMIT = 60 << 20
RADIX = 16


def rfft(x):
    n=len(x)
    if n==1: return [(x[0],None)]
    if n==2: return [(x[0]+x[1],None),(x[0]-x[1],None)]
    e=rfft(x[0::2]); o=rfft(x[1::2]); h=n//2; out=[None]*(h+1)
    out[0]=(e[0][0]+o[0][0],None); out[h]=(e[0][0]-o[0][0],None)
    for k in range(1,h//2):
        c,s=math.cos(2*math.pi*k/n),math.sin(2*math.pi*k/n)
        re,im=o[k]
        if 8*k==n:
            tr=(re+im)*c; ti=(im-re)*c
        else:
            tr=re*c+im*s; ti=im*c-re*s
        out[k]=(e[k][0]+tr,e[k][1]+ti); out[h-k]=(e[k][0]-tr,ti-e[k][1])
    out[h//2]=(e[h//2][0],-o[h//2][0])
    return out

def irfft(X):
    h=len(X)-1; n=2*h
    if h==0: return [X[0][0]]
    if h==1: return [X[0][0]+X[1][0],X[0][0]-X[1][0]]
    E=[None]*(h//2+1); O=[None]*(h//2+1)
    E[0]=(X[0][0]+X[h][0],None); O[0]=(X[0][0]-X[h][0],None)
    for k in range(1,h//2):
        c,s=math.cos(2*math.pi*k/n),math.sin(2*math.pi*k/n)
        (ar,ai),(br,bi)=X[k],X[h-k]
        E[k]=(ar+br,ai-bi)
        dr,di=ar-br,ai+bi
        if 8*k==n: O[k]=((dr-di)*c,(dr+di)*c)
        else: O[k]=(dr*c-di*s,dr*s+di*c)
    r,i=X[h//2]
    E[h//2]=(2.0*r,None); O[h//2]=(-2.0*i,None)
    ev=irfft(E); od=irfft(O); out=[None]*n
    out[0::2]=ev; out[1::2]=od
    return out


def tables(A, W):
    i = np.arange(W)
    ang = 2 * np.pi * (np.outer(i, i) % W) / W
    c, s = np.cos(ang), np.sin(ang)
    m = np.block([[c, -s], [s, c]]).astype(np.float32)
    hi = m.astype(jnp.bfloat16)
    lo = (m - hi.astype(np.float32)).astype(jnp.bfloat16)
    t = 2 * np.pi * np.outer(np.arange(A // 2 + 1), i) / (A * W)
    tw = np.concatenate([np.cos(t), np.sin(t)], 0).astype(np.float32)
    tw = np.concatenate([tw, np.zeros((-len(tw) % 8, W), np.float32)], 0)
    return np.concatenate([hi, lo], 0), tw


def split(z):
    hi = z.astype(bf)
    return hi, (z - hi.astype(f32)).astype(bf)


def onehot(h_ref, bt, W):
    it = lax.broadcasted_iota(jnp.int32, (W, 128), 0).astype(f32).astype(bf)
    one, zero = jnp.ones((W, 128), bf), jnp.zeros((W, 128), bf)
    for j in range(h_ref.shape[0]):
        b = (h_ref[j : j + 1, :] & (W - 1)).astype(f32).astype(bf)
        bt[:, j * 128 : (j + 1) * 128] = jnp.where(it == jnp.broadcast_to(b, (W, 128)), one, zero)


def count(x, h_ref, s_ref, bt, A, W):
    cols = []
    for j in range(h_ref.shape[0]):
        sg = (2 * s_ref[j : j + 1, :] - 1).astype(f32).astype(bf)
        a = lax.shift_right_logical(h_ref[j : j + 1, :], W.bit_length() - 1).astype(f32).astype(bf)
        xs = x[:, j * 128 : (j + 1) * 128] * sg
        ab = jnp.broadcast_to(a, xs.shape)
        z = jnp.zeros_like(xs)
        cols.append(jnp.concatenate([jnp.where(ab == jnp.asarray(k, bf), xs, z) for k in range(A)], 0))
    return lax.dot_general(jnp.concatenate(cols, 1), bt[...], NT, preferred_element_type=f32)


def class_rows(cnt, q, T, tw, z, row0, A, W):
    H = A // 2 + 1
    for t in range(0, T, 8):
        for l in range(0, W, 128):
            planes = [cnt[k, pl.ds(pl.multiple_of(q * T + t, 8), 8), l : l + 128] for k in range(A)]
            for n, (re, im) in enumerate(rfft(planes)):
                if n:
                    c, s = tw[n : n + 1, l : l + 128], tw[H + n : H + n + 1, l : l + 128]
                    re, im = (re * c, -re * s) if im is None else (re * c + im * s, im * c - re * s)
                else:
                    im = jnp.zeros_like(re)
                r = slice(row0 + n * T + t, row0 + n * T + t + 8)
                z[r, l : l + 128] = re
                z[r, W + l : W + l + 128] = im


def dft(z, m, W):
    hi, lo = split(z)
    lhs = jnp.concatenate([hi, lo, hi], 1)
    out = []
    for o in (0, W):
        m_hi, m_lo = m[: 2 * W, o : o + W], m[2 * W :, o : o + W]
        out.append(jnp.dot(lhs, jnp.concatenate([m_hi, m_hi, m_lo], 0), preferred_element_type=f32))
    return out


def kernel(x_hbm, y_hbm, hi_hbm, si_hbm, ho_hbm, so_hbm, m_hbm, tw_hbm, o_ref,
           x, h, s, m, tw, bt, cnt, za, zb, p, sem, *, Q, T, A, W):
    H, R = A // 2 + 1, Q * T
    for i, pairs in enumerate((((hi_hbm, h), (si_hbm, s), (x_hbm, x)), ((ho_hbm, h), (so_hbm, s), (y_hbm, x)))):
        for j, (a, b) in enumerate(pairs):
            pltpu.make_async_copy(a, b.at[i], sem.at[i, j]).start()
    tables_in = [pltpu.make_async_copy(tw_hbm, tw, sem.at[2, 0]), pltpu.make_async_copy(m_hbm, m, sem.at[2, 1])]
    for c in tables_in:
        c.start()
    p[...] = jnp.zeros_like(p)

    def counts(i, carry):
        for j, (a, b) in enumerate(((hi_hbm, h), (si_hbm, s), (x_hbm, x))):
            pltpu.make_async_copy(a, b.at[i], sem.at[i, j]).wait()
        onehot(h.at[i], bt, W)
        cnt[i] = count(x.at[i], h.at[i], s.at[i], bt, A, W).reshape(A, R, W)
        return carry

    lax.fori_loop(0, 2, counts, 0)
    for c in tables_in:
        c.wait()

    def rows(q, z):
        for i in range(2):
            class_rows(cnt.at[i], q, T, tw, z, i * H * T, A, W)

    def product(q, z):
        re, im = dft(z[...], m, W)
        here = lax.broadcasted_iota(jnp.int32, (8, W), 0) == q
        for k in range(H):
            a, b = slice(k * T, (k + 1) * T), slice((H + k) * T, (H + k + 1) * T)
            pr = jnp.sum(re[a] * re[b] - im[a] * im[b], 0, keepdims=True)
            pi = jnp.sum(re[a] * im[b] + im[a] * re[b], 0, keepdims=True)
            r = slice(8 * k, 8 * k + 8)
            p[r, :W] = jnp.where(here, jnp.broadcast_to(pr, (8, W)), p[r, :W])
            p[r, W:] = jnp.where(here, jnp.broadcast_to(pi, (8, W)), p[r, W:])

    rows(0, za)

    def two(j, carry):
        rows(2 * j + 1, zb)
        product(2 * j, za)
        rows(jnp.minimum(2 * j + 2, Q - 1), za)
        product(2 * j + 1, zb)
        return carry

    lax.fori_loop(0, Q // 2, two, 0)
    for k, v in enumerate(back(p[...], m, tw, A, W)):
        o_ref[:, k * W : (k + 1) * W] = v[:Q].astype(o_ref.dtype)


def back(p, m, tw, A, W):
    H = A // 2 + 1
    scale = 1.0 / (A * W)
    re_all, im_all = dft(p * jnp.where(lax.broadcasted_iota(jnp.int32, p.shape, 1) < W, scale, -scale), m, W)
    X = []
    for k in range(H):
        re, im = re_all[8 * k : 8 * k + 8], -im_all[8 * k : 8 * k + 8]
        if k == 0:
            X.append((re, None))
            continue
        c, s = tw[k : k + 1, :], tw[H + k : H + k + 1, :]
        X.append((re * c - im * s, None if k == A // 2 else re * s + im * c))
    return irfft(X)


def sketch(x, y, hash_in, sign_in, hash_out, sign_out, width):
    Q, T, D = x.shape
    assert Q <= 8 and Q % 2 == 0 and y.shape[2] == D
    A, W = RADIX, width // RADIX
    H, R = A // 2 + 1, Q * T
    m, tw = (jnp.asarray(v) for v in tables(A, W))
    hs = [v.reshape(-1, 128) for v in (hash_in, sign_in, hash_out, sign_out)]
    x, y = x.reshape(R, D), y.reshape(R, -1)
    any_ = pl.BlockSpec(memory_space=pl.ANY)
    return pl.pallas_call(
        functools.partial(kernel, Q=Q, T=T, A=A, W=W),
        out_shape=jax.ShapeDtypeStruct((Q, width), bf),
        in_specs=[any_] * 8,
        out_specs=pl.BlockSpec(memory_space=pltpu.VMEM),
        scratch_shapes=[
            pltpu.VMEM((2, R, D), bf), pltpu.VMEM((2, D // 128, 128), jnp.int32), pltpu.VMEM((2, D // 128, 128), jnp.int32),
            pltpu.VMEM(m.shape, bf), pltpu.VMEM(tw.shape, f32),
            pltpu.VMEM((W, D), bf), pltpu.VMEM((2, A, R, W), f32), pltpu.VMEM((2 * H * T, 2 * W), f32), pltpu.VMEM((2 * H * T, 2 * W), f32),
            pltpu.VMEM((H * 8, 2 * W), f32), pltpu.SemaphoreType.DMA((3, 3)),
        ],
        cost_estimate=pl.CostEstimate(flops=4 * R * D * width, bytes_accessed=4 << 20, transcendentals=0),
        compiler_params=pltpu.CompilerParams(vmem_limit_bytes=VMEM_LIMIT),
    )(x, y, *hs, m, tw)


def score_kernel(me_ref, sk_ref, near_ref, far_ref, s_ref, t_ref, *, bits, e):
    q = sk_ref.shape[0]
    rows = jnp.concatenate([near_ref[...], far_ref[...]], 0)
    s = lax.dot_general(sk_ref[...], rows, NT, preferred_element_type=f32)
    t_ref[...] = jnp.sum(s, 0, keepdims=True)
    count = rows.shape[0]
    p = lax.broadcasted_iota(jnp.int32, (count, count), 0)
    shift = e.bit_length() - 1
    device = jnp.broadcast_to(me_ref[0], p.shape)
    for i, bit in enumerate(bits):
        device = device ^ (((p >> (shift + i)) & 1) * bit)
    place = (device << shift) | (p & (e - 1))
    move = jnp.where(place == lax.broadcasted_iota(jnp.int32, p.shape, 1), 1.0, 0.0).astype(bf)
    hi = s.astype(bf)
    rest = s - hi.astype(f32)
    mid = rest.astype(bf)
    low = (rest - mid.astype(f32)).astype(bf)
    moved = [jnp.dot(v, move, preferred_element_type=f32) for v in (hi, mid, low)]
    s_ref[...] = moved[0] + (moved[1] + moved[2])


def score(me, sk, near, far, bits):
    q, e = sk.shape[0], near.shape[0] * 2 >> len(bits)
    total = near.shape[0] * 2
    assert e & (e - 1) == 0
    vm = pl.BlockSpec(memory_space=pltpu.VMEM)
    return pl.pallas_call(
        functools.partial(score_kernel, bits=bits, e=e),
        out_shape=(jax.ShapeDtypeStruct((q, total), f32), jax.ShapeDtypeStruct((1, total), f32)),
        in_specs=[pl.BlockSpec(memory_space=pltpu.SMEM), vm, vm, vm],
        out_specs=(vm, vm),
        cost_estimate=pl.CostEstimate(flops=2 * q * total * sk.shape[1], bytes_accessed=near.size * 4, transcendentals=0),
        compiler_params=pltpu.CompilerParams(vmem_limit_bytes=16 << 20),
    )(me.reshape(1), sk, near, far)


def swap(v, bit, n):
    return lax.ppermute(v, "store", [(i, i ^ bit) for i in range(n)])


def body(query_inputs, query_grads, hash_in, sign_in, hash_out, sign_out, stored):
    n = lax.axis_size("store")
    q_dev, e = query_inputs.shape[0], stored.shape[0]
    bits = [1 << b for b in reversed(range(n.bit_length() - 1))]
    rows = stored
    for bit in bits[:-2]:
        rows = jnp.concatenate([rows, swap(rows, bit, n)], 0)
    rows, hash_in = lax.optimization_barrier((rows, hash_in))
    other = swap(rows, bits[-2], n)
    sk = sketch(query_inputs, query_grads, hash_in, sign_in, hash_out, sign_out, stored.shape[1])
    rows = jnp.concatenate([rows, other], 0)
    scores, t = score(lax.axis_index("store"), sk, rows, swap(rows, bits[-1], n), bits)
    t = t.reshape(-1)
    for bit in reversed(bits):
        half = t.shape[0] // 2
        t = t[:half] + swap(t[half:], bit, n)
    return scores, t / (n * q_dev)


def solution(mesh):
    rows = P(("grp", "store"), None)
    cube = P(("grp", "store"), None, None)
    return jax.shard_map(
        body,
        mesh=mesh,
        in_specs=(cube, cube, P(), P(), P(), P(), rows),
        out_specs=(rows, P(("grp", "store"))),
        check_vma=False,
    )
```

```python
import functools, math
import numpy as np
import jax, jax.numpy as jnp
from jax import lax
from jax.experimental import pallas as pl
from jax.experimental.pallas import tpu as pltpu
from jax.sharding import PartitionSpec as P

bf = jnp.bfloat16
f32 = jnp.float32
NT = (((1,), (1,)), ((), ()))
VMEM_LIMIT = 28 << 20
RADIX = 16


def rfft(x):
    n=len(x)
    if n==1: return [(x[0],None)]
    if n==2: return [(x[0]+x[1],None),(x[0]-x[1],None)]
    e=rfft(x[0::2]); o=rfft(x[1::2]); h=n//2; out=[None]*(h+1)
    out[0]=(e[0][0]+o[0][0],None); out[h]=(e[0][0]-o[0][0],None)
    for k in range(1,h//2):
        c,s=math.cos(2*math.pi*k/n),math.sin(2*math.pi*k/n)
        re,im=o[k]
        if 8*k==n:
            tr=(re+im)*c; ti=(im-re)*c
        else:
            tr=re*c+im*s; ti=im*c-re*s
        out[k]=(e[k][0]+tr,e[k][1]+ti); out[h-k]=(e[k][0]-tr,ti-e[k][1])
    out[h//2]=(e[h//2][0],-o[h//2][0])
    return out

def irfft(X):
    h=len(X)-1; n=2*h
    if h==0: return [X[0][0]]
    if h==1: return [X[0][0]+X[1][0],X[0][0]-X[1][0]]
    E=[None]*(h//2+1); O=[None]*(h//2+1)
    E[0]=(X[0][0]+X[h][0],None); O[0]=(X[0][0]-X[h][0],None)
    for k in range(1,h//2):
        c,s=math.cos(2*math.pi*k/n),math.sin(2*math.pi*k/n)
        (ar,ai),(br,bi)=X[k],X[h-k]
        E[k]=(ar+br,ai-bi)
        dr,di=ar-br,ai+bi
        if 8*k==n: O[k]=((dr-di)*c,(dr+di)*c)
        else: O[k]=(dr*c-di*s,dr*s+di*c)
    r,i=X[h//2]
    E[h//2]=(2.0*r,None); O[h//2]=(-2.0*i,None)
    ev=irfft(E); od=irfft(O); out=[None]*n
    out[0::2]=ev; out[1::2]=od
    return out


def tables(A, W):
    i = np.arange(W)
    ang = 2 * np.pi * (np.outer(i, i) % W) / W
    c, s = np.cos(ang), np.sin(ang)
    m = np.block([[c, -s], [s, c]]).astype(np.float32)
    hi = m.astype(jnp.bfloat16)
    lo = (m - hi.astype(np.float32)).astype(jnp.bfloat16)
    t = 2 * np.pi * np.outer(np.arange(A // 2 + 1), i) / (A * W)
    tw = np.concatenate([np.cos(t), np.sin(t)], 0).astype(np.float32)
    tw = np.concatenate([tw, np.zeros((-len(tw) % 8, W), np.float32)], 0)
    return np.concatenate([hi, lo], 0), tw


def split(z):
    hi = z.astype(bf)
    return hi, (z - hi.astype(f32)).astype(bf)


def onehot(h_ref, bt, W):
    it = lax.broadcasted_iota(jnp.int32, (W, 128), 0).astype(f32).astype(bf)
    one, zero = jnp.ones((W, 128), bf), jnp.zeros((W, 128), bf)
    for j in range(h_ref.shape[0]):
        b = (h_ref[j : j + 1, :] & (W - 1)).astype(f32).astype(bf)
        bt[:, j * 128 : (j + 1) * 128] = jnp.where(it == jnp.broadcast_to(b, (W, 128)), one, zero)


def count(x, h_ref, s_ref, bt, A, W):
    cols = []
    for j in range(h_ref.shape[0]):
        sg = (2 * s_ref[j : j + 1, :] - 1).astype(f32).astype(bf)
        a = lax.shift_right_logical(h_ref[j : j + 1, :], W.bit_length() - 1).astype(f32).astype(bf)
        xs = x[:, j * 128 : (j + 1) * 128] * sg
        ab = jnp.broadcast_to(a, xs.shape)
        z = jnp.zeros_like(xs)
        cols.append(jnp.concatenate([jnp.where(ab == jnp.asarray(k, bf), xs, z) for k in range(A)], 0))
    return lax.dot_general(jnp.concatenate(cols, 1), bt[...], NT, preferred_element_type=f32)


def class_rows(cnt, q, T, tw, z, row0, A, W):
    H = A // 2 + 1
    for t in range(0, T, 8):
        for l in range(0, W, 128):
            planes = [cnt[k, pl.ds(pl.multiple_of(q * T + t, 8), 8), l : l + 128] for k in range(A)]
            for n, (re, im) in enumerate(rfft(planes)):
                if n:
                    c, s = tw[n : n + 1, l : l + 128], tw[H + n : H + n + 1, l : l + 128]
                    re, im = (re * c, -re * s) if im is None else (re * c + im * s, im * c - re * s)
                else:
                    im = jnp.zeros_like(re)
                r = slice(row0 + n * T + t, row0 + n * T + t + 8)
                z[r, l : l + 128] = re
                z[r, W + l : W + l + 128] = im


def dft(z, m, W):
    hi, lo = split(z)
    lhs = jnp.concatenate([hi, lo, hi], 1)
    out = []
    for o in (0, W):
        m_hi, m_lo = m[: 2 * W, o : o + W], m[2 * W :, o : o + W]
        out.append(jnp.dot(lhs, jnp.concatenate([m_hi, m_hi, m_lo], 0), preferred_element_type=f32))
    return out


def kernel(x, y, hi, si, ho, so, m, tw, o_ref, bt, cx, cy, zx, zy, fr, fi, p, *, Q, T, A, W):
    H, R = A // 2 + 1, Q * T
    p[...] = jnp.zeros_like(p)

    def counts(rows_ref, h, s, cnt):
        onehot(h, bt, W)
        cnt[...] = count(rows_ref, h, s, bt, A, W).reshape(A, R, W)

    def rows(cnt, z, q0, q1):
        for q in range(q0, q1):
            class_rows(cnt, q, T, tw, z, q * H * T, A, W)

    def transform(q0, q1):
        r = slice(q0 * H * T, q1 * H * T)
        fr[r, :], fi[r, :] = dft(zx[r, :], m, W)

    def product(q0, q1):
        re, im = dft(zy[q0 * H * T : q1 * H * T, :], m, W)
        for q in range(q0, q1):
            here = lax.broadcasted_iota(jnp.int32, (8, W), 0) == q
            for k in range(H):
                a = slice((q * H + k) * T, (q * H + k + 1) * T)
                b = slice(((q - q0) * H + k) * T, ((q - q0) * H + k + 1) * T)
                pr = jnp.sum(fr[a, :] * re[b] - fi[a, :] * im[b], 0, keepdims=True)
                pi = jnp.sum(fr[a, :] * im[b] + fi[a, :] * re[b], 0, keepdims=True)
                r = slice(8 * k, 8 * k + 8)
                p[r, :W] = jnp.where(here, jnp.broadcast_to(pr, (8, W)), p[r, :W])
                p[r, W:] = jnp.where(here, jnp.broadcast_to(pi, (8, W)), p[r, W:])

    counts(x, hi, si, cx)
    counts(y, ho, so, cy)
    rows(cx, zx, 0, Q)
    rows(cy, zy, 0, Q)
    transform(0, Q)
    product(0, Q)
    for k, v in enumerate(back(p[...], m, tw, A, W)):
        o_ref[:, k * W : (k + 1) * W] = v[:Q].astype(o_ref.dtype)


def back(p, m, tw, A, W):
    H = A // 2 + 1
    scale = 1.0 / (A * W)
    re_all, im_all = dft(p * jnp.where(lax.broadcasted_iota(jnp.int32, p.shape, 1) < W, scale, -scale), m, W)
    X = []
    for k in range(H):
        re, im = re_all[8 * k : 8 * k + 8], -im_all[8 * k : 8 * k + 8]
        if k == 0:
            X.append((re, None))
            continue
        c, s = tw[k : k + 1, :], tw[H + k : H + k + 1, :]
        X.append((re * c - im * s, None if k == A // 2 else re * s + im * c))
    return irfft(X)


def sketch(x, y, hash_in, sign_in, hash_out, sign_out, width):
    Q, T, D = x.shape
    A, W = RADIX, width // RADIX
    H, R = A // 2 + 1, Q * T
    assert Q <= 8
    m, tw = (jnp.asarray(v) for v in tables(A, W))
    hs = [v.reshape(-1, 128) for v in (hash_in, sign_in, hash_out, sign_out)]
    vm = pl.BlockSpec(memory_space=pltpu.VMEM)
    return pl.pallas_call(
        functools.partial(kernel, Q=Q, T=T, A=A, W=W),
        out_shape=jax.ShapeDtypeStruct((Q, width), bf),
        in_specs=[vm] * 8,
        out_specs=vm,
        scratch_shapes=[
            pltpu.VMEM((W, D), bf), pltpu.VMEM((A, R, W), f32), pltpu.VMEM((A, R, W), f32),
            pltpu.VMEM((Q * H * T, 2 * W), f32), pltpu.VMEM((Q * H * T, 2 * W), f32),
            pltpu.VMEM((Q * H * T, W), f32), pltpu.VMEM((Q * H * T, W), f32), pltpu.VMEM((H * 8, 2 * W), f32),
        ],
        cost_estimate=pl.CostEstimate(flops=4 * R * D * width, bytes_accessed=4 << 20, transcendentals=0),
        compiler_params=pltpu.CompilerParams(vmem_limit_bytes=VMEM_LIMIT),
    )(x.reshape(R, D), y.reshape(R, -1), *hs, m, tw)


def score_kernel(me_ref, sk_ref, near_ref, far_ref, s_ref, t_ref, *, bits, e):
    q = sk_ref.shape[0]
    rows = jnp.concatenate([near_ref[...], far_ref[...]], 0)
    s = lax.dot_general(sk_ref[...], rows, NT, preferred_element_type=f32)
    t_ref[...] = jnp.sum(s, 0, keepdims=True)
    count = rows.shape[0]
    p = lax.broadcasted_iota(jnp.int32, (count, count), 0)
    shift = e.bit_length() - 1
    device = jnp.broadcast_to(me_ref[0], p.shape)
    for i, bit in enumerate(bits):
        device = device ^ (((p >> (shift + i)) & 1) * bit)
    place = (device << shift) | (p & (e - 1))
    move = jnp.where(place == lax.broadcasted_iota(jnp.int32, p.shape, 1), 1.0, 0.0).astype(bf)
    hi = s.astype(bf)
    rest = s - hi.astype(f32)
    mid = rest.astype(bf)
    low = (rest - mid.astype(f32)).astype(bf)
    moved = [jnp.dot(v, move, preferred_element_type=f32) for v in (hi, mid, low)]
    s_ref[...] = moved[0] + (moved[1] + moved[2])


def score(me, sk, near, far, bits):
    q, e = sk.shape[0], near.shape[0] * 2 >> len(bits)
    total = near.shape[0] * 2
    assert e & (e - 1) == 0
    vm = pl.BlockSpec(memory_space=pltpu.VMEM)
    return pl.pallas_call(
        functools.partial(score_kernel, bits=bits, e=e),
        out_shape=(jax.ShapeDtypeStruct((q, total), f32), jax.ShapeDtypeStruct((1, total), f32)),
        in_specs=[pl.BlockSpec(memory_space=pltpu.SMEM), vm, vm, vm],
        out_specs=(vm, vm),
        cost_estimate=pl.CostEstimate(flops=2 * q * total * sk.shape[1], bytes_accessed=near.size * 4, transcendentals=0),
        compiler_params=pltpu.CompilerParams(vmem_limit_bytes=16 << 20),
    )(me.reshape(1), sk, near, far)


def swap(v, bit, n):
    return lax.ppermute(v, "store", [(i, i ^ bit) for i in range(n)])


def body(query_inputs, query_grads, hash_in, sign_in, hash_out, sign_out, stored):
    n = lax.axis_size("store")
    q_dev, e = query_inputs.shape[0], stored.shape[0]
    bits = [1 << b for b in reversed(range(n.bit_length() - 1))]
    bits = bits[:-2] + [1, 2]
    rows = stored
    for bit in bits[:-1]:
        rows = jnp.concatenate([rows, swap(rows, bit, n)], 0)
    rows, hash_in = lax.optimization_barrier((rows, hash_in))
    far = swap(rows, bits[-1], n)
    sk = sketch(query_inputs, query_grads, hash_in, sign_in, hash_out, sign_out, stored.shape[1])
    scores, t = score(lax.axis_index("store"), sk, rows, far, bits)
    t = t.reshape(-1)
    for bit in reversed(bits):
        half = t.shape[0] // 2
        t = t[:half] + swap(t[half:], bit, n)
    return scores, t / (n * q_dev)


def solution(mesh):
    rows = P(("grp", "store"), None)
    cube = P(("grp", "store"), None, None)
    return jax.shard_map(
        body,
        mesh=mesh,
        in_specs=(cube, cube, P(), P(), P(), P(), rows),
        out_specs=(rows, P(("grp", "store"))),
        check_vma=False,
    )
```

```python
import functools, math
import numpy as np
import jax, jax.numpy as jnp
from jax import lax
from jax.experimental import pallas as pl
from jax.experimental.pallas import tpu as pltpu
from jax.sharding import PartitionSpec as P

bf = jnp.bfloat16
f32 = jnp.float32
NT = (((1,), (1,)), ((), ()))
VMEM_LIMIT = 24 << 20
RADIX = 16


def rfft(x):
    n=len(x)
    if n==1: return [(x[0],None)]
    if n==2: return [(x[0]+x[1],None),(x[0]-x[1],None)]
    e=rfft(x[0::2]); o=rfft(x[1::2]); h=n//2; out=[None]*(h+1)
    out[0]=(e[0][0]+o[0][0],None); out[h]=(e[0][0]-o[0][0],None)
    for k in range(1,h//2):
        c,s=math.cos(2*math.pi*k/n),math.sin(2*math.pi*k/n)
        re,im=o[k]
        if 8*k==n:
            tr=(re+im)*c; ti=(im-re)*c
        else:
            tr=re*c+im*s; ti=im*c-re*s
        out[k]=(e[k][0]+tr,e[k][1]+ti); out[h-k]=(e[k][0]-tr,ti-e[k][1])
    out[h//2]=(e[h//2][0],-o[h//2][0])
    return out

def irfft(X):
    h=len(X)-1; n=2*h
    if h==0: return [X[0][0]]
    if h==1: return [X[0][0]+X[1][0],X[0][0]-X[1][0]]
    E=[None]*(h//2+1); O=[None]*(h//2+1)
    E[0]=(X[0][0]+X[h][0],None); O[0]=(X[0][0]-X[h][0],None)
    for k in range(1,h//2):
        c,s=math.cos(2*math.pi*k/n),math.sin(2*math.pi*k/n)
        (ar,ai),(br,bi)=X[k],X[h-k]
        E[k]=(ar+br,ai-bi)
        dr,di=ar-br,ai+bi
        if 8*k==n: O[k]=((dr-di)*c,(dr+di)*c)
        else: O[k]=(dr*c-di*s,dr*s+di*c)
    r,i=X[h//2]
    E[h//2]=(2.0*r,None); O[h//2]=(-2.0*i,None)
    ev=irfft(E); od=irfft(O); out=[None]*n
    out[0::2]=ev; out[1::2]=od
    return out


def tables(A, W):
    i = np.arange(W)
    ang = 2 * np.pi * (np.outer(i, i) % W) / W
    c, s = np.cos(ang), np.sin(ang)
    m = np.block([[c, -s], [s, c]]).astype(np.float32)
    hi = m.astype(jnp.bfloat16)
    lo = (m - hi.astype(np.float32)).astype(jnp.bfloat16)
    t = 2 * np.pi * np.outer(np.arange(A // 2 + 1), i) / (A * W)
    tw = np.concatenate([np.cos(t), np.sin(t)], 0).astype(np.float32)
    tw = np.concatenate([tw, np.zeros((-len(tw) % 8, W), np.float32)], 0)
    return np.concatenate([hi, lo], 0), tw


def split(z):
    hi = z.astype(bf)
    return hi, (z - hi.astype(f32)).astype(bf)


def onehot(h_ref, bt, W):
    it = lax.broadcasted_iota(jnp.int32, (W, 128), 0).astype(f32).astype(bf)
    one, zero = jnp.ones((W, 128), bf), jnp.zeros((W, 128), bf)
    for j in range(h_ref.shape[0]):
        b = (h_ref[j : j + 1, :] & (W - 1)).astype(f32).astype(bf)
        bt[:, j * 128 : (j + 1) * 128] = jnp.where(it == jnp.broadcast_to(b, (W, 128)), one, zero)


def count(x, h_ref, s_ref, bt, A, W):
    cols = []
    for j in range(h_ref.shape[0]):
        sg = (2 * s_ref[j : j + 1, :] - 1).astype(f32).astype(bf)
        a = lax.shift_right_logical(h_ref[j : j + 1, :], W.bit_length() - 1).astype(f32).astype(bf)
        xs = x[:, j * 128 : (j + 1) * 128] * sg
        ab = jnp.broadcast_to(a, xs.shape)
        z = jnp.zeros_like(xs)
        cols.append(jnp.concatenate([jnp.where(ab == jnp.asarray(k, bf), xs, z) for k in range(A)], 0))
    return lax.dot_general(jnp.concatenate(cols, 1), bt[...], NT, preferred_element_type=f32)


def class_rows(cnt, q, T, tw, z, row0, A, W):
    H = A // 2 + 1
    for t in range(0, T, 8):
        for l in range(0, W, 128):
            planes = [cnt[k, pl.ds(pl.multiple_of(q * T + t, 8), 8), l : l + 128] for k in range(A)]
            for n, (re, im) in enumerate(rfft(planes)):
                if n:
                    c, s = tw[n : n + 1, l : l + 128], tw[H + n : H + n + 1, l : l + 128]
                    re, im = (re * c, -re * s) if im is None else (re * c + im * s, im * c - re * s)
                else:
                    im = jnp.zeros_like(re)
                r = slice(row0 + n * T + t, row0 + n * T + t + 8)
                z[r, l : l + 128] = re
                z[r, W + l : W + l + 128] = im


def dft(z, m, W):
    hi, lo = split(z)
    lhs = jnp.concatenate([hi, lo, hi], 1)
    out = []
    for o in (0, W):
        m_hi, m_lo = m[: 2 * W, o : o + W], m[2 * W :, o : o + W]
        out.append(jnp.dot(lhs, jnp.concatenate([m_hi, m_hi, m_lo], 0), preferred_element_type=f32))
    return out


def count_kernel(*refs, Q, T, A, W):
    given, (cx, cy, x, y, hi, si, ho, so, bt, sem) = refs[:6], refs[6:]
    copies = [pltpu.make_async_copy(a, b, sem.at[i]) for i, (a, b) in enumerate(zip(given, (hi, si, x, ho, so, y)))]
    for c in copies:
        c.start()
    for c in copies:
        c.wait()
    for rows_ref, h, s, cnt in ((x, hi, si, cx), (y, ho, so, cy)):
        onehot(h, bt, W)
        cnt[...] = count(rows_ref, h, s, bt, A, W).reshape(A, Q * T, W)


def sketch_kernel(cx, cy, m, tw, o_ref, zx, zy, fr, fi, p, *, Q, T, A, W):
    H = A // 2 + 1
    p[...] = jnp.zeros_like(p)
    for cnt, z in ((cx, zx), (cy, zy)):
        for q in range(Q):
            class_rows(cnt, q, T, tw, z, q * H * T, A, W)
    fr[...], fi[...] = dft(zx[...], m, W)
    re, im = dft(zy[...], m, W)
    for q in range(Q):
        here = lax.broadcasted_iota(jnp.int32, (8, W), 0) == q
        for k in range(H):
            a = slice((q * H + k) * T, (q * H + k + 1) * T)
            pr = jnp.sum(fr[a, :] * re[a] - fi[a, :] * im[a], 0, keepdims=True)
            pi = jnp.sum(fr[a, :] * im[a] + fi[a, :] * re[a], 0, keepdims=True)
            r = slice(8 * k, 8 * k + 8)
            p[r, :W] = jnp.where(here, jnp.broadcast_to(pr, (8, W)), p[r, :W])
            p[r, W:] = jnp.where(here, jnp.broadcast_to(pi, (8, W)), p[r, W:])
    for k, v in enumerate(back(p[...], m, tw, A, W)):
        o_ref[:, k * W : (k + 1) * W] = v[:Q].astype(o_ref.dtype)


def back(p, m, tw, A, W):
    H = A // 2 + 1
    scale = 1.0 / (A * W)
    re_all, im_all = dft(p * jnp.where(lax.broadcasted_iota(jnp.int32, p.shape, 1) < W, scale, -scale), m, W)
    X = []
    for k in range(H):
        re, im = re_all[8 * k : 8 * k + 8], -im_all[8 * k : 8 * k + 8]
        if k == 0:
            X.append((re, None))
            continue
        c, s = tw[k : k + 1, :], tw[H + k : H + k + 1, :]
        X.append((re * c - im * s, None if k == A // 2 else re * s + im * c))
    return irfft(X)


def counts(x, y, hash_in, sign_in, hash_out, sign_out, width):
    Q, T, D = x.shape
    A, W = RADIX, width // RADIX
    hi, si, ho, so = (v.reshape(-1, 128) for v in (hash_in, sign_in, hash_out, sign_out))
    x, y = x.reshape(Q * T, D), y.reshape(Q * T, -1)
    vm = pl.BlockSpec(memory_space=pltpu.VMEM)
    return pl.pallas_call(
        functools.partial(count_kernel, Q=Q, T=T, A=A, W=W),
        out_shape=(jax.ShapeDtypeStruct((A, Q * T, W), f32),) * 2,
        in_specs=[pl.BlockSpec(memory_space=pltpu.HBM)] * 6,
        out_specs=(vm, vm),
        scratch_shapes=[pltpu.VMEM(v.shape, v.dtype) for v in (x, y, hi, si, ho, so)] + [pltpu.VMEM((W, D), bf), pltpu.SemaphoreType.DMA((6,))],
        cost_estimate=pl.CostEstimate(flops=4 * Q * T * D * width, bytes_accessed=4 << 20, transcendentals=0),
        compiler_params=pltpu.CompilerParams(vmem_limit_bytes=VMEM_LIMIT),
    )(*(pltpu.with_memory_space_constraint(v, pltpu.HBM) for v in (hi, si, x, ho, so, y)))


def sketch(cx, cy, Q):
    A, R, W = cx.shape
    T, H = R // Q, A // 2 + 1
    assert Q <= 8
    m, tw = (jnp.asarray(v) for v in tables(A, W))
    vm = pl.BlockSpec(memory_space=pltpu.VMEM)
    return pl.pallas_call(
        functools.partial(sketch_kernel, Q=Q, T=T, A=A, W=W),
        out_shape=jax.ShapeDtypeStruct((Q, A * W), bf),
        in_specs=[vm] * 4,
        out_specs=vm,
        scratch_shapes=[
            pltpu.VMEM((Q * H * T, 2 * W), f32), pltpu.VMEM((Q * H * T, 2 * W), f32),
            pltpu.VMEM((Q * H * T, W), f32), pltpu.VMEM((Q * H * T, W), f32), pltpu.VMEM((H * 8, 2 * W), f32),
        ],
        cost_estimate=pl.CostEstimate(flops=1 << 32, bytes_accessed=4 << 20, transcendentals=0),
        compiler_params=pltpu.CompilerParams(vmem_limit_bytes=VMEM_LIMIT),
    )(cx, cy, m, tw)


def score_kernel(me_ref, sk_ref, near_ref, far_ref, s_ref, t_ref, *, bits, e):
    q = sk_ref.shape[0]
    rows = jnp.concatenate([near_ref[...], far_ref[...]], 0)
    s = lax.dot_general(sk_ref[...], rows, NT, preferred_element_type=f32)
    t_ref[...] = jnp.sum(s, 0, keepdims=True)
    count = rows.shape[0]
    p = lax.broadcasted_iota(jnp.int32, (count, count), 0)
    shift = e.bit_length() - 1
    device = jnp.broadcast_to(me_ref[0], p.shape)
    for i, bit in enumerate(bits):
        device = device ^ (((p >> (shift + i)) & 1) * bit)
    place = (device << shift) | (p & (e - 1))
    move = jnp.where(place == lax.broadcasted_iota(jnp.int32, p.shape, 1), 1.0, 0.0).astype(bf)
    hi = s.astype(bf)
    rest = s - hi.astype(f32)
    mid = rest.astype(bf)
    low = (rest - mid.astype(f32)).astype(bf)
    moved = [jnp.dot(v, move, preferred_element_type=f32) for v in (hi, mid, low)]
    s_ref[...] = moved[0] + (moved[1] + moved[2])


def score(me, sk, near, far, bits):
    q, e = sk.shape[0], near.shape[0] * 2 >> len(bits)
    total = near.shape[0] * 2
    assert e & (e - 1) == 0
    vm = pl.BlockSpec(memory_space=pltpu.VMEM)
    return pl.pallas_call(
        functools.partial(score_kernel, bits=bits, e=e),
        out_shape=(jax.ShapeDtypeStruct((q, total), f32), jax.ShapeDtypeStruct((1, total), f32)),
        in_specs=[pl.BlockSpec(memory_space=pltpu.SMEM), vm, vm, vm],
        out_specs=(vm, vm),
        cost_estimate=pl.CostEstimate(flops=2 * q * total * sk.shape[1], bytes_accessed=near.size * 4, transcendentals=0),
        compiler_params=pltpu.CompilerParams(vmem_limit_bytes=16 << 20),
    )(me.reshape(1), sk, near, far)


def swap(v, bit, n):
    return lax.ppermute(v, "store", [(i, i ^ bit) for i in range(n)])


def body(query_inputs, query_grads, hash_in, sign_in, hash_out, sign_out, stored):
    n = lax.axis_size("store")
    q_dev, e = query_inputs.shape[0], stored.shape[0]
    bits = [1 << b for b in reversed(range(n.bit_length() - 1))]
    first, second = bits[:2]
    parts = [stored] + [swap(stored, bit, n) for bit in (first, second, first ^ second)]
    cx, cy = counts(query_inputs, query_grads, hash_in, sign_in, hash_out, sign_out, stored.shape[1])
    rows, cx = lax.optimization_barrier((jnp.concatenate(parts, 0), cx))
    for bit in bits[2:-2]:
        rows = jnp.concatenate([rows, swap(rows, bit, n)], 0)
    other = swap(rows, bits[-2], n)
    sk = sketch(cx, cy, q_dev)
    rows, sk = lax.optimization_barrier((jnp.concatenate([rows, other], 0), sk))
    scores, t = score(lax.axis_index("store"), sk, rows, swap(rows, bits[-1], n), bits)
    t = t.reshape(-1)
    for bit in reversed(bits):
        half = t.shape[0] // 2
        t = t[:half] + swap(t[half:], bit, n)
    return scores, t / (n * q_dev)


def solution(mesh):
    rows = P(("grp", "store"), None)
    cube = P(("grp", "store"), None, None)
    return jax.shard_map(
        body,
        mesh=mesh,
        in_specs=(cube, cube, P(), P(), P(), P(), rows),
        out_specs=(rows, P(("grp", "store"))),
        check_vma=False,
    )
```

```python
import functools, math
import numpy as np
import jax, jax.numpy as jnp
from jax import lax
from jax.experimental import pallas as pl
from jax.experimental.pallas import tpu as pltpu
from jax.sharding import PartitionSpec as P

bf = jnp.bfloat16
f32 = jnp.float32
NT = (((1,), (1,)), ((), ()))
VMEM_LIMIT = 24 << 20
RADIX = 16


def rfft(x):
    n=len(x)
    if n==1: return [(x[0],None)]
    if n==2: return [(x[0]+x[1],None),(x[0]-x[1],None)]
    e=rfft(x[0::2]); o=rfft(x[1::2]); h=n//2; out=[None]*(h+1)
    out[0]=(e[0][0]+o[0][0],None); out[h]=(e[0][0]-o[0][0],None)
    for k in range(1,h//2):
        c,s=math.cos(2*math.pi*k/n),math.sin(2*math.pi*k/n)
        re,im=o[k]
        if 8*k==n:
            tr=(re+im)*c; ti=(im-re)*c
        else:
            tr=re*c+im*s; ti=im*c-re*s
        out[k]=(e[k][0]+tr,e[k][1]+ti); out[h-k]=(e[k][0]-tr,ti-e[k][1])
    out[h//2]=(e[h//2][0],-o[h//2][0])
    return out

def irfft(X):
    h=len(X)-1; n=2*h
    if h==0: return [X[0][0]]
    if h==1: return [X[0][0]+X[1][0],X[0][0]-X[1][0]]
    E=[None]*(h//2+1); O=[None]*(h//2+1)
    E[0]=(X[0][0]+X[h][0],None); O[0]=(X[0][0]-X[h][0],None)
    for k in range(1,h//2):
        c,s=math.cos(2*math.pi*k/n),math.sin(2*math.pi*k/n)
        (ar,ai),(br,bi)=X[k],X[h-k]
        E[k]=(ar+br,ai-bi)
        dr,di=ar-br,ai+bi
        if 8*k==n: O[k]=((dr-di)*c,(dr+di)*c)
        else: O[k]=(dr*c-di*s,dr*s+di*c)
    r,i=X[h//2]
    E[h//2]=(2.0*r,None); O[h//2]=(-2.0*i,None)
    ev=irfft(E); od=irfft(O); out=[None]*n
    out[0::2]=ev; out[1::2]=od
    return out


def tables(A, W):
    i = np.arange(W)
    ang = 2 * np.pi * (np.outer(i, i) % W) / W
    c, s = np.cos(ang), np.sin(ang)
    m = np.block([[c, -s], [s, c]]).astype(np.float32)
    hi = m.astype(jnp.bfloat16)
    lo = (m - hi.astype(np.float32)).astype(jnp.bfloat16)
    t = 2 * np.pi * np.outer(np.arange(A // 2 + 1), i) / (A * W)
    tw = np.concatenate([np.cos(t), np.sin(t)], 0).astype(np.float32)
    tw = np.concatenate([tw, np.zeros((-len(tw) % 8, W), np.float32)], 0)
    return np.concatenate([hi, lo], 0), tw


def split(z):
    hi = z.astype(bf)
    return hi, (z - hi.astype(f32)).astype(bf)


def onehot(h_ref, bt, W):
    it = lax.broadcasted_iota(jnp.int32, (W, 128), 0).astype(f32).astype(bf)
    one, zero = jnp.ones((W, 128), bf), jnp.zeros((W, 128), bf)
    for j in range(h_ref.shape[0]):
        b = (h_ref[j : j + 1, :] & (W - 1)).astype(f32).astype(bf)
        bt[:, j * 128 : (j + 1) * 128] = jnp.where(it == jnp.broadcast_to(b, (W, 128)), one, zero)


def count(x, h_ref, s_ref, bt, A, W):
    cols = []
    for j in range(h_ref.shape[0]):
        sg = (2 * s_ref[j : j + 1, :] - 1).astype(f32).astype(bf)
        a = lax.shift_right_logical(h_ref[j : j + 1, :], W.bit_length() - 1).astype(f32).astype(bf)
        xs = x[:, j * 128 : (j + 1) * 128] * sg
        ab = jnp.broadcast_to(a, xs.shape)
        z = jnp.zeros_like(xs)
        cols.append(jnp.concatenate([jnp.where(ab == jnp.asarray(k, bf), xs, z) for k in range(A)], 0))
    return lax.dot_general(jnp.concatenate(cols, 1), bt[...], NT, preferred_element_type=f32)


def class_rows(cnt, base, R, q, T, tw, z, row0, A, W):
    H = A // 2 + 1
    for t in range(0, T, 8):
        for l in range(0, W, 128):
            starts = [base + k * R + q * T + t for k in range(A)]
            planes = [cnt[i : i + 8, l : l + 128] for i in starts]
            for n, (re, im) in enumerate(rfft(planes)):
                if n:
                    c, s = tw[n : n + 1, l : l + 128], tw[H + n : H + n + 1, l : l + 128]
                    re, im = (re * c, -re * s) if im is None else (re * c + im * s, im * c - re * s)
                else:
                    im = jnp.zeros_like(re)
                r = slice(row0 + n * T + t, row0 + n * T + t + 8)
                z[r, l : l + 128] = re
                z[r, W + l : W + l + 128] = im


def dft(z, m, W):
    hi, lo = split(z)
    lhs = jnp.concatenate([hi, lo, hi], 1)
    out = []
    for o in (0, W):
        m_hi, m_lo = m[: 2 * W, o : o + W], m[2 * W :, o : o + W]
        out.append(jnp.dot(lhs, jnp.concatenate([m_hi, m_hi, m_lo], 0), preferred_element_type=f32))
    return out


def first_kernel(*refs, A, W):
    given, (cx, y, ho, so, x, hi, si, bt, sem) = refs[:6], refs[6:]
    copies = [pltpu.make_async_copy(a, b, sem.at[i]) for i, (a, b) in enumerate(zip(given, (hi, si, x, ho, so, y)))]
    for c in copies:
        c.start()
    for c in copies:
        c.wait()
    onehot(hi, bt, W)
    cx[...] = count(x, hi, si, bt, A, W)


def second_kernel(cx, y, ho, so, m, tw, out, zx, bt, *, Q, T, A, W):
    H, R = A // 2 + 1, Q * T
    for q in range(Q):
        class_rows(cx, 0, R, q, T, tw, zx, q * H * T, A, W)
    out[: H * R, :], out[H * R : 2 * H * R, :] = dft(zx[...], m, W)
    onehot(ho, bt, W)
    out[2 * H * R :, :] = count(y, ho, so, bt, A, W)


def third_kernel(f, m, tw, o_ref, zy, p, *, Q, T, A, W):
    H, R = A // 2 + 1, Q * T
    p[...] = jnp.zeros_like(p)
    for q in range(Q):
        class_rows(f, 2 * H * R, R, q, T, tw, zy, q * H * T, A, W)
    re, im = dft(zy[...], m, W)
    for q in range(Q):
        here = lax.broadcasted_iota(jnp.int32, (8, W), 0) == q
        for k in range(H):
            a = slice((q * H + k) * T, (q * H + k + 1) * T)
            fr, fi = f[a, :], f[H * R + a.start : H * R + a.stop, :]
            pr = jnp.sum(fr * re[a] - fi * im[a], 0, keepdims=True)
            pi = jnp.sum(fr * im[a] + fi * re[a], 0, keepdims=True)
            r = slice(8 * k, 8 * k + 8)
            p[r, :W] = jnp.where(here, jnp.broadcast_to(pr, (8, W)), p[r, :W])
            p[r, W:] = jnp.where(here, jnp.broadcast_to(pi, (8, W)), p[r, W:])
    for k, v in enumerate(back(p[...], m, tw, A, W)):
        o_ref[:, k * W : (k + 1) * W] = v[:Q].astype(o_ref.dtype)


def back(p, m, tw, A, W):
    H = A // 2 + 1
    scale = 1.0 / (A * W)
    re_all, im_all = dft(p * jnp.where(lax.broadcasted_iota(jnp.int32, p.shape, 1) < W, scale, -scale), m, W)
    X = []
    for k in range(H):
        re, im = re_all[8 * k : 8 * k + 8], -im_all[8 * k : 8 * k + 8]
        if k == 0:
            X.append((re, None))
            continue
        c, s = tw[k : k + 1, :], tw[H + k : H + k + 1, :]
        X.append((re * c - im * s, None if k == A // 2 else re * s + im * c))
    return irfft(X)


def call(kernel, out, args, scratch, flops, spec=pltpu.VMEM):
    vm = pl.BlockSpec(memory_space=pltpu.VMEM)
    return pl.pallas_call(
        kernel,
        out_shape=out,
        in_specs=[pl.BlockSpec(memory_space=spec)] * len(args),
        out_specs=jax.tree.map(lambda _: vm, out),
        scratch_shapes=scratch,
        cost_estimate=pl.CostEstimate(flops=flops, bytes_accessed=4 << 20, transcendentals=0),
        compiler_params=pltpu.CompilerParams(vmem_limit_bytes=VMEM_LIMIT),
    )(*args)


def first(x, y, hi, si, ho, so, A, W):
    R, D = x.shape
    like = lambda v: jax.ShapeDtypeStruct(v.shape, v.dtype)
    args = [pltpu.with_memory_space_constraint(v, pltpu.HBM) for v in (hi, si, x, ho, so, y)]
    scratch = [pltpu.VMEM(v.shape, v.dtype) for v in (x, hi, si)] + [pltpu.VMEM((W, D), bf), pltpu.SemaphoreType.DMA((6,))]
    out = (jax.ShapeDtypeStruct((A * R, W), f32), like(y), like(ho), like(so))
    return call(functools.partial(first_kernel, A=A, W=W), out, args, scratch, 2 * R * D * A * W, pltpu.HBM)


def second(cx, y, ho, so, m, tw, Q, A):
    W = cx.shape[1]
    R = cx.shape[0] // A
    rows = R * (A // 2 + 1)
    out = jax.ShapeDtypeStruct((2 * rows + A * R, W), f32)
    scratch = [pltpu.VMEM((rows, 2 * W), f32), pltpu.VMEM((W, y.shape[1]), bf)]
    return call(functools.partial(second_kernel, Q=Q, T=R // Q, A=A, W=W), out, (cx, y, ho, so, m, tw), scratch, 2 * R * y.shape[1] * A * W)


def third(f, m, tw, Q, R, A):
    W, H = f.shape[1], A // 2 + 1
    assert Q <= 8
    out = jax.ShapeDtypeStruct((Q, A * W), bf)
    scratch = [pltpu.VMEM((R * H, 2 * W), f32), pltpu.VMEM((H * 8, 2 * W), f32)]
    return call(functools.partial(third_kernel, Q=Q, T=R // Q, A=A, W=W), out, (f, m, tw), scratch, 1 << 31)


def score_kernel(me_ref, sk_ref, *refs, bits, e, n):
    parts, (s_ref, t_ref) = refs[:-2], refs[-2:]
    rows = jnp.concatenate([r[...] for r in parts], 0)
    s = lax.dot_general(sk_ref[...], rows, NT, preferred_element_type=f32)
    count = n * e
    shift = e.bit_length() - 1

    def device_of(p):
        device = jnp.broadcast_to(me_ref[0], p.shape)
        for i, bit in enumerate(bits):
            device = device ^ (((p >> (shift + i)) & 1) * bit)
        return device

    def thirds(v):
        hi = v.astype(bf)
        rest = v - hi.astype(f32)
        mid = rest.astype(bf)
        return hi, mid, (rest - mid.astype(f32)).astype(bf)

    def pick(v, m):
        hi, mid, low = (jnp.dot(u, m, preferred_element_type=f32) for u in thirds(v))
        return hi + (mid + low)

    def ones_where(m):
        return jnp.where(m, 1.0, 0.0).astype(bf)

    def iota(shape, d):
        return lax.broadcasted_iota(jnp.int32, shape, d)

    p = iota((count, count), 0)
    place = (device_of(p) << shift) | (p & (e - 1))
    s_ref[...] = pick(s, ones_where(place == iota((count, count), 1)))
    sums = jnp.broadcast_to(jnp.sum(s, 0, keepdims=True), (n, count))
    mine = jnp.where(device_of(iota((n, count), 1)) == iota((n, count), 0), sums, 0.0)
    t_ref[...] = pick(mine, ones_where((iota((count, e), 0) & (e - 1)) == iota((count, e), 1)))


def score(me, sk, parts, bits, n):
    q, total = sk.shape[0], sum(v.shape[0] for v in parts)
    e = total // n
    assert e & (e - 1) == 0
    vm = pl.BlockSpec(memory_space=pltpu.VMEM)
    return pl.pallas_call(
        functools.partial(score_kernel, bits=bits, e=e, n=n),
        out_shape=(jax.ShapeDtypeStruct((q, total), f32), jax.ShapeDtypeStruct((n, e), f32)),
        in_specs=[pl.BlockSpec(memory_space=pltpu.SMEM)] + [vm] * (1 + len(parts)),
        out_specs=(vm, vm),
        cost_estimate=pl.CostEstimate(flops=2 * q * total * sk.shape[1], bytes_accessed=total * 8192, transcendentals=0),
        compiler_params=pltpu.CompilerParams(vmem_limit_bytes=16 << 20),
    )(me.reshape(1), sk, *parts)


def swap(v, bit, n):
    return lax.ppermute(v, "store", [(i, i ^ bit) for i in range(n)])


def body(query_inputs, query_grads, hash_in, sign_in, hash_out, sign_out, stored):
    n = lax.axis_size("store")
    q_dev, e = query_inputs.shape[0], stored.shape[0]
    bits = [1 << b for b in reversed(range(n.bit_length() - 1))]
    b0, b1 = bits[:2]
    parts = [stored] + [swap(stored, bit, n) for bit in (b0, b1, b0 ^ b1)]
    A, width = RADIX, stored.shape[1]
    m, tw = (jnp.asarray(v) for v in tables(A, width // A))
    tokens = q_dev * query_inputs.shape[1]
    tabs = (v.reshape(-1, 128) for v in (hash_in, sign_in, hash_out, sign_out))
    cx, *rest = first(query_inputs.reshape(tokens, -1), query_grads.reshape(tokens, -1), *tabs, A, width // A)
    rows, cx = lax.optimization_barrier((jnp.concatenate(parts, 0), cx))
    for bit in bits[2:-2]:
        rows = jnp.concatenate([rows, swap(rows, bit, n)], 0)
    across = swap(rows, bits[-2], n)
    twin = swap(rows, bits[-1], n)
    f = second(cx, *rest, m, tw, q_dev, A)
    across, f = lax.optimization_barrier((across, f))
    twin_across = swap(across, bits[-1], n)
    sk = third(f, m, tw, q_dev, tokens, A)
    scores, t = score(lax.axis_index("store"), sk, [rows, across, twin, twin_across], bits, n)
    totals = jnp.sum(lax.all_to_all(t, "store", 0, 0), 0)
    return scores, totals / (n * q_dev)


def solution(mesh):
    rows = P(("grp", "store"), None)
    cube = P(("grp", "store"), None, None)
    return jax.shard_map(
        body,
        mesh=mesh,
        in_specs=(cube, cube, P(), P(), P(), P(), rows),
        out_specs=(rows, P(("grp", "store"))),
        check_vma=False,
    )
```

```python
import functools, math
import numpy as np
import jax, jax.numpy as jnp
from jax import lax
from jax.experimental import pallas as pl
from jax.experimental.pallas import tpu as pltpu
from jax.sharding import PartitionSpec as P

bf = jnp.bfloat16
f32 = jnp.float32
NT = (((1,), (1,)), ((), ()))
VMEM_LIMIT = 24 << 20
RADIX = 16


def rfft(x):
    n=len(x)
    if n==1: return [(x[0],None)]
    if n==2: return [(x[0]+x[1],None),(x[0]-x[1],None)]
    e=rfft(x[0::2]); o=rfft(x[1::2]); h=n//2; out=[None]*(h+1)
    out[0]=(e[0][0]+o[0][0],None); out[h]=(e[0][0]-o[0][0],None)
    for k in range(1,h//2):
        c,s=math.cos(2*math.pi*k/n),math.sin(2*math.pi*k/n)
        re,im=o[k]
        if 8*k==n:
            tr=(re+im)*c; ti=(im-re)*c
        else:
            tr=re*c+im*s; ti=im*c-re*s
        out[k]=(e[k][0]+tr,e[k][1]+ti); out[h-k]=(e[k][0]-tr,ti-e[k][1])
    out[h//2]=(e[h//2][0],-o[h//2][0])
    return out

def irfft(X):
    h=len(X)-1; n=2*h
    if h==0: return [X[0][0]]
    if h==1: return [X[0][0]+X[1][0],X[0][0]-X[1][0]]
    E=[None]*(h//2+1); O=[None]*(h//2+1)
    E[0]=(X[0][0]+X[h][0],None); O[0]=(X[0][0]-X[h][0],None)
    for k in range(1,h//2):
        c,s=math.cos(2*math.pi*k/n),math.sin(2*math.pi*k/n)
        (ar,ai),(br,bi)=X[k],X[h-k]
        E[k]=(ar+br,ai-bi)
        dr,di=ar-br,ai+bi
        if 8*k==n: O[k]=((dr-di)*c,(dr+di)*c)
        else: O[k]=(dr*c-di*s,dr*s+di*c)
    r,i=X[h//2]
    E[h//2]=(2.0*r,None); O[h//2]=(-2.0*i,None)
    ev=irfft(E); od=irfft(O); out=[None]*n
    out[0::2]=ev; out[1::2]=od
    return out


def tables(A, W):
    i = np.arange(W)
    ang = 2 * np.pi * (np.outer(i, i) % W) / W
    c, s = np.cos(ang), np.sin(ang)
    m = np.block([[c, -s], [s, c]]).astype(np.float32)
    hi = m.astype(jnp.bfloat16)
    lo = (m - hi.astype(np.float32)).astype(jnp.bfloat16)
    t = 2 * np.pi * np.outer(np.arange(A // 2 + 1), i) / (A * W)
    tw = np.concatenate([np.cos(t), np.sin(t)], 0).astype(np.float32)
    tw = np.concatenate([tw, np.zeros((-len(tw) % 8, W), np.float32)], 0)
    return np.concatenate([hi, lo], 0), tw


def split(z):
    hi = z.astype(bf)
    return hi, (z - hi.astype(f32)).astype(bf)


def onehot(h_ref, bt, W):
    it = lax.broadcasted_iota(jnp.int32, (W, 128), 0).astype(f32).astype(bf)
    one, zero = jnp.ones((W, 128), bf), jnp.zeros((W, 128), bf)
    for j in range(h_ref.shape[0]):
        b = (h_ref[j : j + 1, :] & (W - 1)).astype(f32).astype(bf)
        bt[:, j * 128 : (j + 1) * 128] = jnp.where(it == jnp.broadcast_to(b, (W, 128)), one, zero)


def count(x, h_ref, s_ref, bt, A, W):
    cols = []
    for j in range(h_ref.shape[0]):
        sg = (2 * s_ref[j : j + 1, :] - 1).astype(f32).astype(bf)
        a = lax.shift_right_logical(h_ref[j : j + 1, :], W.bit_length() - 1).astype(f32).astype(bf)
        xs = x[:, j * 128 : (j + 1) * 128] * sg
        ab = jnp.broadcast_to(a, xs.shape)
        z = jnp.zeros_like(xs)
        cols.append(jnp.concatenate([jnp.where(ab == jnp.asarray(k, bf), xs, z) for k in range(A)], 0))
    return lax.dot_general(jnp.concatenate(cols, 1), bt[...], NT, preferred_element_type=f32)


def class_rows(cnt, base, R, q, T, tw, z, row0, A, W):
    H = A // 2 + 1
    for t in range(0, T, 8):
        for l in range(0, W, 128):
            starts = [base + k * R + q * T + t for k in range(A)]
            planes = [cnt[i : i + 8, l : l + 128] for i in starts]
            for n, (re, im) in enumerate(rfft(planes)):
                if n:
                    c, s = tw[n : n + 1, l : l + 128], tw[H + n : H + n + 1, l : l + 128]
                    re, im = (re * c, -re * s) if im is None else (re * c + im * s, im * c - re * s)
                else:
                    im = jnp.zeros_like(re)
                r = slice(row0 + n * T + t, row0 + n * T + t + 8)
                z[r, l : l + 128] = re
                z[r, W + l : W + l + 128] = im


def dft(z, m, W):
    hi, lo = split(z)
    lhs = jnp.concatenate([hi, lo, hi], 1)
    out = []
    for o in (0, W):
        m_hi, m_lo = m[: 2 * W, o : o + W], m[2 * W :, o : o + W]
        out.append(jnp.dot(lhs, jnp.concatenate([m_hi, m_hi, m_lo], 0), preferred_element_type=f32))
    return out


def first_kernel(*refs, A, W):
    given, (cx, y, ho, so, x, hi, si, bt, sem) = refs[:6], refs[6:]
    copies = [pltpu.make_async_copy(a, b, sem.at[i]) for i, (a, b) in enumerate(zip(given, (hi, si, x, ho, so, y)))]
    for c in copies:
        c.start()
    for c in copies[:3]:
        c.wait()
    onehot(hi, bt, W)
    cx[...] = count(x, hi, si, bt, A, W)
    for c in copies[3:]:
        c.wait()


def second_kernel(cx, y, ho, so, m, tw, fr, fi, zy, zx, cy, bt, *, Q, T, A, W):
    H, R = A // 2 + 1, Q * T
    for q in range(Q):
        class_rows(cx, 0, R, q, T, tw, zx, q * H * T, A, W)
    onehot(ho, bt, W)
    cy[...] = count(y, ho, so, bt, A, W)
    for q in range(Q):
        class_rows(cy, 0, R, q, T, tw, zy, q * H * T, A, W)
    fr[...], fi[...] = dft(zx[...], m, W)


def third_kernel(fr, fi, zy, m, tw, o_ref, p, *, Q, T, A, W):
    H = A // 2 + 1
    p[...] = jnp.zeros_like(p)
    re, im = dft(zy[...], m, W)
    for q in range(Q):
        here = lax.broadcasted_iota(jnp.int32, (8, W), 0) == q
        for k in range(H):
            a = slice((q * H + k) * T, (q * H + k + 1) * T)
            ar, ai = fr[a, :], fi[a, :]
            pr = jnp.sum(ar * re[a] - ai * im[a], 0, keepdims=True)
            pi = jnp.sum(ar * im[a] + ai * re[a], 0, keepdims=True)
            r = slice(8 * k, 8 * k + 8)
            p[r, :W] = jnp.where(here, jnp.broadcast_to(pr, (8, W)), p[r, :W])
            p[r, W:] = jnp.where(here, jnp.broadcast_to(pi, (8, W)), p[r, W:])
    for k, v in enumerate(back(p[...], m, tw, A, W)):
        o_ref[:, k * W : (k + 1) * W] = v[:Q].astype(o_ref.dtype)


def back(p, m, tw, A, W):
    H = A // 2 + 1
    scale = 1.0 / (A * W)
    re_all, im_all = dft(p * jnp.where(lax.broadcasted_iota(jnp.int32, p.shape, 1) < W, scale, -scale), m, W)
    X = []
    for k in range(H):
        re, im = re_all[8 * k : 8 * k + 8], -im_all[8 * k : 8 * k + 8]
        if k == 0:
            X.append((re, None))
            continue
        c, s = tw[k : k + 1, :], tw[H + k : H + k + 1, :]
        X.append((re * c - im * s, None if k == A // 2 else re * s + im * c))
    return irfft(X)


def call(kernel, out, args, scratch, flops, spec=pltpu.VMEM):
    vm = pl.BlockSpec(memory_space=pltpu.VMEM)
    return pl.pallas_call(
        kernel,
        out_shape=out,
        in_specs=[pl.BlockSpec(memory_space=spec)] * len(args),
        out_specs=jax.tree.map(lambda _: vm, out),
        scratch_shapes=scratch,
        cost_estimate=pl.CostEstimate(flops=flops, bytes_accessed=4 << 20, transcendentals=0),
        compiler_params=pltpu.CompilerParams(vmem_limit_bytes=VMEM_LIMIT),
    )(*args)


def first(x, y, hi, si, ho, so, A, W):
    R, D = x.shape
    like = lambda v: jax.ShapeDtypeStruct(v.shape, v.dtype)
    args = [pltpu.with_memory_space_constraint(v, pltpu.HBM) for v in (hi, si, x, ho, so, y)]
    scratch = [pltpu.VMEM(v.shape, v.dtype) for v in (x, hi, si)] + [pltpu.VMEM((W, D), bf), pltpu.SemaphoreType.DMA((6,))]
    out = (jax.ShapeDtypeStruct((A * R, W), f32), like(y), like(ho), like(so))
    return call(functools.partial(first_kernel, A=A, W=W), out, args, scratch, 2 * R * D * A * W, pltpu.HBM)


def second(cx, y, ho, so, m, tw, Q, A):
    W = cx.shape[1]
    R = cx.shape[0] // A
    rows = R * (A // 2 + 1)
    out = (jax.ShapeDtypeStruct((rows, W), f32),) * 2 + (jax.ShapeDtypeStruct((rows, 2 * W), f32),)
    scratch = [pltpu.VMEM((rows, 2 * W), f32), pltpu.VMEM(cx.shape, f32), pltpu.VMEM((W, y.shape[1]), bf)]
    return call(functools.partial(second_kernel, Q=Q, T=R // Q, A=A, W=W), out, (cx, y, ho, so, m, tw), scratch, 2 * R * y.shape[1] * A * W)


def third(fr, fi, zy, m, tw, Q, R, A):
    W, H = fr.shape[1], A // 2 + 1
    assert Q <= 8
    out = jax.ShapeDtypeStruct((Q, A * W), bf)
    return call(functools.partial(third_kernel, Q=Q, T=R // Q, A=A, W=W), out, (fr, fi, zy, m, tw), [pltpu.VMEM((H * 8, 2 * W), f32)], 1 << 31)


def score_kernel(me_ref, sk_ref, *refs, bits, e, n):
    parts, (s_ref, t_ref) = refs[:-2], refs[-2:]
    rows = jnp.concatenate([r[...] for r in parts], 0)
    s = lax.dot_general(sk_ref[...], rows, NT, preferred_element_type=f32)
    count = n * e
    shift = e.bit_length() - 1

    def device_of(p):
        block = p >> shift
        device = (me_ref[0] - (block & 3) * (n // 4)) & (n - 1)
        for i, bit in enumerate(bits[2:], 2):
            device = device ^ (((block >> i) & 1) * bit)
        return device

    def thirds(v):
        hi = v.astype(bf)
        rest = v - hi.astype(f32)
        mid = rest.astype(bf)
        return hi, mid, (rest - mid.astype(f32)).astype(bf)

    def pick(v, m):
        hi, mid, low = (jnp.dot(u, m, preferred_element_type=f32) for u in thirds(v))
        return hi + (mid + low)

    def ones_where(m):
        return jnp.where(m, 1.0, 0.0).astype(bf)

    def iota(shape, d):
        return lax.broadcasted_iota(jnp.int32, shape, d)

    p = iota((count, count), 0)
    place = (device_of(p) << shift) | (p & (e - 1))
    s_ref[...] = pick(s, ones_where(place == iota((count, count), 1)))
    sums = jnp.broadcast_to(jnp.sum(s, 0, keepdims=True), (n, count))
    mine = jnp.where(device_of(iota((n, count), 1)) == iota((n, count), 0), sums, 0.0)
    t_ref[...] = pick(mine, ones_where((iota((count, e), 0) & (e - 1)) == iota((count, e), 1)))


def score(me, sk, parts, bits, n):
    q, total = sk.shape[0], sum(v.shape[0] for v in parts)
    e = total // n
    assert e & (e - 1) == 0
    vm = pl.BlockSpec(memory_space=pltpu.VMEM)
    return pl.pallas_call(
        functools.partial(score_kernel, bits=bits, e=e, n=n),
        out_shape=(jax.ShapeDtypeStruct((q, total), f32), jax.ShapeDtypeStruct((n, e), f32)),
        in_specs=[pl.BlockSpec(memory_space=pltpu.SMEM)] + [vm] * (1 + len(parts)),
        out_specs=(vm, vm),
        cost_estimate=pl.CostEstimate(flops=2 * q * total * sk.shape[1], bytes_accessed=total * 8192, transcendentals=0),
        compiler_params=pltpu.CompilerParams(vmem_limit_bytes=16 << 20),
    )(me.reshape(1), sk, *parts)


def swap(v, bit, n):
    return lax.ppermute(v, "store", [(i, i ^ bit) for i in range(n)])


def turn(v, step, n):
    return lax.ppermute(v, "store", [(i, (i + step) % n) for i in range(n)])


def body(query_inputs, query_grads, hash_in, sign_in, hash_out, sign_out, stored):
    n = lax.axis_size("store")
    q_dev, e = query_inputs.shape[0], stored.shape[0]
    bits = [1 << b for b in reversed(range(n.bit_length() - 1))]
    parts = [turn(stored, k * n // 4, n) for k in (3, 2, 1)]
    parts = [stored] + parts[::-1]
    A, width = RADIX, stored.shape[1]
    m, tw = (jnp.asarray(v) for v in tables(A, width // A))
    tokens = q_dev * query_inputs.shape[1]
    tabs = (v.reshape(-1, 128) for v in (hash_in, sign_in, hash_out, sign_out))
    cx, *rest = first(query_inputs.reshape(tokens, -1), query_grads.reshape(tokens, -1), *tabs, A, width // A)
    rows, cx = lax.optimization_barrier((jnp.concatenate(parts, 0), cx))
    for bit in bits[2:-2]:
        rows = jnp.concatenate([rows, swap(rows, bit, n)], 0)
    across = swap(rows, bits[-2], n)
    twin = swap(rows, bits[-1], n)
    fr, fi, zy = second(cx, *rest, m, tw, q_dev, A)
    across, zy = lax.optimization_barrier((across, zy))
    twin_across = swap(across, bits[-1], n)
    sk = third(fr, fi, zy, m, tw, q_dev, tokens, A)
    scores, t = score(lax.axis_index("store"), sk, [rows, across, twin, twin_across], bits, n)
    totals = jnp.sum(lax.all_to_all(t, "store", 0, 0), 0)
    return scores, totals / (n * q_dev)


def solution(mesh):
    rows = P(("grp", "store"), None)
    cube = P(("grp", "store"), None, None)
    return jax.shard_map(
        body,
        mesh=mesh,
        in_specs=(cube, cube, P(), P(), P(), P(), rows),
        out_specs=(rows, P(("grp", "store"))),
        check_vma=False,
    )
```

```python
import functools, math
import numpy as np
import jax, jax.numpy as jnp
from jax import lax
from jax.experimental import pallas as pl
from jax.experimental.pallas import tpu as pltpu
from jax.sharding import PartitionSpec as P

bf = jnp.bfloat16
f32 = jnp.float32
NT = (((1,), (1,)), ((), ()))
VMEM_LIMIT = 24 << 20
RADIX = 16


def rfft(x):
    n=len(x)
    if n==1: return [(x[0],None)]
    if n==2: return [(x[0]+x[1],None),(x[0]-x[1],None)]
    e=rfft(x[0::2]); o=rfft(x[1::2]); h=n//2; out=[None]*(h+1)
    out[0]=(e[0][0]+o[0][0],None); out[h]=(e[0][0]-o[0][0],None)
    for k in range(1,h//2):
        c,s=math.cos(2*math.pi*k/n),math.sin(2*math.pi*k/n)
        re,im=o[k]
        if 8*k==n:
            tr=(re+im)*c; ti=(im-re)*c
        else:
            tr=re*c+im*s; ti=im*c-re*s
        out[k]=(e[k][0]+tr,e[k][1]+ti); out[h-k]=(e[k][0]-tr,ti-e[k][1])
    out[h//2]=(e[h//2][0],-o[h//2][0])
    return out

def irfft(X):
    h=len(X)-1; n=2*h
    if h==0: return [X[0][0]]
    if h==1: return [X[0][0]+X[1][0],X[0][0]-X[1][0]]
    E=[None]*(h//2+1); O=[None]*(h//2+1)
    E[0]=(X[0][0]+X[h][0],None); O[0]=(X[0][0]-X[h][0],None)
    for k in range(1,h//2):
        c,s=math.cos(2*math.pi*k/n),math.sin(2*math.pi*k/n)
        (ar,ai),(br,bi)=X[k],X[h-k]
        E[k]=(ar+br,ai-bi)
        dr,di=ar-br,ai+bi
        if 8*k==n: O[k]=((dr-di)*c,(dr+di)*c)
        else: O[k]=(dr*c-di*s,dr*s+di*c)
    r,i=X[h//2]
    E[h//2]=(2.0*r,None); O[h//2]=(-2.0*i,None)
    ev=irfft(E); od=irfft(O); out=[None]*n
    out[0::2]=ev; out[1::2]=od
    return out


def tables(A, W):
    i = np.arange(W)
    ang = 2 * np.pi * (np.outer(i, i) % W) / W
    c, s = np.cos(ang), np.sin(ang)
    m = np.block([[c, -s], [s, c]]).astype(np.float32)
    hi = m.astype(jnp.bfloat16)
    lo = (m - hi.astype(np.float32)).astype(jnp.bfloat16)
    t = 2 * np.pi * np.outer(np.arange(A // 2 + 1), i) / (A * W)
    tw = np.concatenate([np.cos(t), np.sin(t)], 0).astype(np.float32)
    tw = np.concatenate([tw, np.zeros((-len(tw) % 8, W), np.float32)], 0)
    return np.concatenate([hi, lo], 0), tw


def split(z):
    hi = z.astype(bf)
    return hi, (z - hi.astype(f32)).astype(bf)


def onehot(h_ref, bt, W):
    it = lax.broadcasted_iota(jnp.int32, (W, 128), 0).astype(f32).astype(bf)
    one, zero = jnp.ones((W, 128), bf), jnp.zeros((W, 128), bf)
    for j in range(h_ref.shape[0]):
        b = (h_ref[j : j + 1, :] & (W - 1)).astype(f32).astype(bf)
        bt[:, j * 128 : (j + 1) * 128] = jnp.where(it == jnp.broadcast_to(b, (W, 128)), one, zero)


def count(x, h_ref, s_ref, bt, A, W):
    cols = []
    for j in range(h_ref.shape[0]):
        sg = (2 * s_ref[j : j + 1, :] - 1).astype(f32).astype(bf)
        a = lax.shift_right_logical(h_ref[j : j + 1, :], W.bit_length() - 1).astype(f32).astype(bf)
        xs = x[:, j * 128 : (j + 1) * 128] * sg
        ab = jnp.broadcast_to(a, xs.shape)
        z = jnp.zeros_like(xs)
        cols.append(jnp.concatenate([jnp.where(ab == jnp.asarray(k, bf), xs, z) for k in range(A)], 0))
    return lax.dot_general(jnp.concatenate(cols, 1), bt[...], NT, preferred_element_type=f32)


def class_rows(cnt, base, R, q, T, tw, z, row0, A, W):
    H = A // 2 + 1
    for t in range(0, T, 8):
        for l in range(0, W, 128):
            starts = [base + k * R + q * T + t for k in range(A)]
            planes = [cnt[i : i + 8, l : l + 128] for i in starts]
            for n, (re, im) in enumerate(rfft(planes)):
                if n:
                    c, s = tw[n : n + 1, l : l + 128], tw[H + n : H + n + 1, l : l + 128]
                    re, im = (re * c, -re * s) if im is None else (re * c + im * s, im * c - re * s)
                else:
                    im = jnp.zeros_like(re)
                r = slice(row0 + n * T + t, row0 + n * T + t + 8)
                z[r, l : l + 128] = re
                z[r, W + l : W + l + 128] = im


def dft(z, m, W):
    hi, lo = split(z)
    lhs = jnp.concatenate([hi, lo, hi], 1)
    out = []
    for o in (0, W):
        m_hi, m_lo = m[: 2 * W, o : o + W], m[2 * W :, o : o + W]
        out.append(jnp.dot(lhs, jnp.concatenate([m_hi, m_hi, m_lo], 0), preferred_element_type=f32))
    return out


def first_kernel(*refs, Q, T, A, W):
    given, (zx, y, ho, so, x, hi, si, tw, bt, cx, sem) = refs[:7], refs[7:]
    copies = [pltpu.make_async_copy(a, b, sem.at[i]) for i, (a, b) in enumerate(zip(given, (hi, si, x, tw, ho, so, y)))]
    for c in copies:
        c.start()
    copies[0].wait()
    onehot(hi, bt, W)
    for c in copies[1:4]:
        c.wait()
    cx[...] = count(x, hi, si, bt, A, W)
    for q in range(Q):
        class_rows(cx, 0, Q * T, q, T, tw, zx, q * (A // 2 + 1) * T, A, W)
    for c in copies[4:]:
        c.wait()


def second_kernel(zx, y, ho, so, m, tw, fr, fi, zy, cy, bt, *, Q, T, A, W):
    H, R = A // 2 + 1, Q * T
    onehot(ho, bt, W)
    cy[...] = count(y, ho, so, bt, A, W)
    for q in range(Q):
        class_rows(cy, 0, R, q, T, tw, zy, q * H * T, A, W)
    fr[...], fi[...] = dft(zx[...], m, W)


def third_kernel(fr, fi, zy, m, tw, o_ref, p, *, Q, T, A, W):
    H = A // 2 + 1
    p[...] = jnp.zeros_like(p)
    re, im = dft(zy[...], m, W)
    for q in range(Q):
        here = lax.broadcasted_iota(jnp.int32, (8, W), 0) == q
        for k in range(H):
            a = slice((q * H + k) * T, (q * H + k + 1) * T)
            ar, ai = fr[a, :], fi[a, :]
            pr = jnp.sum(ar * re[a] - ai * im[a], 0, keepdims=True)
            pi = jnp.sum(ar * im[a] + ai * re[a], 0, keepdims=True)
            r = slice(8 * k, 8 * k + 8)
            p[r, :W] = jnp.where(here, jnp.broadcast_to(pr, (8, W)), p[r, :W])
            p[r, W:] = jnp.where(here, jnp.broadcast_to(pi, (8, W)), p[r, W:])
    for k, v in enumerate(back(p[...], m, tw, A, W)):
        o_ref[:, k * W : (k + 1) * W] = v[:Q].astype(o_ref.dtype)


def back(p, m, tw, A, W):
    H = A // 2 + 1
    scale = 1.0 / (A * W)
    re_all, im_all = dft(p * jnp.where(lax.broadcasted_iota(jnp.int32, p.shape, 1) < W, scale, -scale), m, W)
    X = []
    for k in range(H):
        re, im = re_all[8 * k : 8 * k + 8], -im_all[8 * k : 8 * k + 8]
        if k == 0:
            X.append((re, None))
            continue
        c, s = tw[k : k + 1, :], tw[H + k : H + k + 1, :]
        X.append((re * c - im * s, None if k == A // 2 else re * s + im * c))
    return irfft(X)


def call(kernel, out, args, scratch, flops, spec=pltpu.VMEM):
    vm = pl.BlockSpec(memory_space=pltpu.VMEM)
    return pl.pallas_call(
        kernel,
        out_shape=out,
        in_specs=[pl.BlockSpec(memory_space=spec)] * len(args),
        out_specs=jax.tree.map(lambda _: vm, out),
        scratch_shapes=scratch,
        cost_estimate=pl.CostEstimate(flops=flops, bytes_accessed=4 << 20, transcendentals=0),
        compiler_params=pltpu.CompilerParams(vmem_limit_bytes=VMEM_LIMIT),
    )(*args)


def first(x, y, hi, si, ho, so, tw, A, Q):
    (R, D), W = x.shape, tw.shape[1]
    like = lambda v: jax.ShapeDtypeStruct(v.shape, v.dtype)
    args = [pltpu.with_memory_space_constraint(v, pltpu.HBM) for v in (hi, si, x, tw, ho, so, y)]
    scratch = [pltpu.VMEM(v.shape, v.dtype) for v in (x, hi, si, tw)] + [pltpu.VMEM((W, D), bf), pltpu.VMEM((A * R, W), f32), pltpu.SemaphoreType.DMA((7,))]
    out = (jax.ShapeDtypeStruct((R * (A // 2 + 1), 2 * W), f32), like(y), like(ho), like(so))
    return call(functools.partial(first_kernel, Q=Q, T=R // Q, A=A, W=W), out, args, scratch, 2 * R * D * A * W, pltpu.HBM)


def second(zx, y, ho, so, m, tw, Q, A):
    rows, W = zx.shape[0], tw.shape[1]
    R = rows // (A // 2 + 1)
    out = (jax.ShapeDtypeStruct((rows, W), f32),) * 2 + (like_rows(rows, W),)
    scratch = [pltpu.VMEM((A * R, W), f32), pltpu.VMEM((W, y.shape[1]), bf)]
    return call(functools.partial(second_kernel, Q=Q, T=R // Q, A=A, W=W), out, (zx, y, ho, so, m, tw), scratch, 2 * R * y.shape[1] * A * W)


def like_rows(rows, W):
    return jax.ShapeDtypeStruct((rows, 2 * W), f32)


def third(fr, fi, zy, m, tw, Q, R, A):
    W, H = fr.shape[1], A // 2 + 1
    assert Q <= 8
    out = jax.ShapeDtypeStruct((Q, A * W), bf)
    return call(functools.partial(third_kernel, Q=Q, T=R // Q, A=A, W=W), out, (fr, fi, zy, m, tw), [pltpu.VMEM((H * 8, 2 * W), f32)], 1 << 31)


def score_kernel(me_ref, sk_ref, *refs, bits, e, n):
    parts, (s_ref, t_ref) = refs[:-2], refs[-2:]
    rows = jnp.concatenate([r[...] for r in parts], 0)
    s = lax.dot_general(sk_ref[...], rows, NT, preferred_element_type=f32)
    count = n * e
    shift = e.bit_length() - 1

    def device_of(p):
        block = p >> shift
        device = (me_ref[0] - (block & 3) * (n // 4)) & (n - 1)
        for i, bit in enumerate(bits[2:], 2):
            device = device ^ (((block >> i) & 1) * bit)
        return device

    def thirds(v):
        hi = v.astype(bf)
        rest = v - hi.astype(f32)
        mid = rest.astype(bf)
        return hi, mid, (rest - mid.astype(f32)).astype(bf)

    def pick(v, m):
        hi, mid, low = (jnp.dot(u, m, preferred_element_type=f32) for u in thirds(v))
        return hi + (mid + low)

    def ones_where(m):
        return jnp.where(m, 1.0, 0.0).astype(bf)

    def iota(shape, d):
        return lax.broadcasted_iota(jnp.int32, shape, d)

    p = iota((count, count), 0)
    place = (device_of(p) << shift) | (p & (e - 1))
    s_ref[...] = pick(s, ones_where(place == iota((count, count), 1)))
    sums = jnp.broadcast_to(jnp.sum(s, 0, keepdims=True), (n, count))
    mine = jnp.where(device_of(iota((n, count), 1)) == iota((n, count), 0), sums, 0.0)
    t_ref[...] = pick(mine, ones_where((iota((count, e), 0) & (e - 1)) == iota((count, e), 1)))


def score(me, sk, parts, bits, n):
    q, total = sk.shape[0], sum(v.shape[0] for v in parts)
    e = total // n
    assert e & (e - 1) == 0
    vm = pl.BlockSpec(memory_space=pltpu.VMEM)
    return pl.pallas_call(
        functools.partial(score_kernel, bits=bits, e=e, n=n),
        out_shape=(jax.ShapeDtypeStruct((q, total), f32), jax.ShapeDtypeStruct((n, e), f32)),
        in_specs=[pl.BlockSpec(memory_space=pltpu.SMEM)] + [vm] * (1 + len(parts)),
        out_specs=(vm, vm),
        cost_estimate=pl.CostEstimate(flops=2 * q * total * sk.shape[1], bytes_accessed=total * 8192, transcendentals=0),
        compiler_params=pltpu.CompilerParams(vmem_limit_bytes=16 << 20),
    )(me.reshape(1), sk, *parts)


def swap(v, bit, n):
    return lax.ppermute(v, "store", [(i, i ^ bit) for i in range(n)])


def turn(v, step, n):
    return lax.ppermute(v, "store", [(i, (i + step) % n) for i in range(n)])


def body(query_inputs, query_grads, hash_in, sign_in, hash_out, sign_out, stored):
    n = lax.axis_size("store")
    q_dev, e = query_inputs.shape[0], stored.shape[0]
    bits = [1 << b for b in reversed(range(n.bit_length() - 1))]
    parts = [turn(stored, k * n // 4, n) for k in (3, 2, 1)]
    parts = [stored] + parts[::-1]
    A, width = RADIX, stored.shape[1]
    m, tw = (jnp.asarray(v) for v in tables(A, width // A))
    tokens = q_dev * query_inputs.shape[1]
    tabs = (v.reshape(-1, 128) for v in (hash_in, sign_in, hash_out, sign_out))
    zx, *rest = first(query_inputs.reshape(tokens, -1), query_grads.reshape(tokens, -1), *tabs, tw, A, q_dev)
    rows, zx = lax.optimization_barrier((jnp.concatenate(parts, 0), zx))
    for bit in bits[2:-2]:
        rows = jnp.concatenate([rows, swap(rows, bit, n)], 0)
    across = swap(rows, bits[-2], n)
    twin = swap(rows, bits[-1], n)
    fr, fi, zy = second(zx, *rest, m, tw, q_dev, A)
    across, zy = lax.optimization_barrier((across, zy))
    twin_across = swap(across, bits[-1], n)
    sk = third(fr, fi, zy, m, tw, q_dev, tokens, A)
    scores, t = score(lax.axis_index("store"), sk, [rows, across, twin, twin_across], bits, n)
    totals = jnp.sum(lax.all_to_all(t, "store", 0, 0), 0)
    return scores, totals / (n * q_dev)


def solution(mesh):
    rows = P(("grp", "store"), None)
    cube = P(("grp", "store"), None, None)
    return jax.shard_map(
        body,
        mesh=mesh,
        in_specs=(cube, cube, P(), P(), P(), P(), rows),
        out_specs=(rows, P(("grp", "store"))),
        check_vma=False,
    )
```
